768 devices in a mesh: ctx: 96 (over z, y_hi, core), head: 4 (over x), scene: 2 (over y_lo).
Axes of the slice: x: 4, y: 8 (y_hi: 4, y_lo: 2; y = y_hi * 2 + y_lo), z: 12, core: 2. Of those that a mesh axis runs over, the one named last changes fastest.
Arguments:
- queries: bfloat16 [2, 15360, 512], P('scene', 'ctx', 'head'), may hold values from -8 to 8
- key_states: bfloat16 [2, 15360, 512], P('scene', 'ctx', 'head'), may hold values from -8 to 8
- value_states: bfloat16 [2, 15360, 512], P('scene', 'ctx', 'head'), may hold values from -6 to 6
- splat_weight: float32 [2, 15360], P('scene', 'ctx'), may hold values from 0.25 to 2.5
- tile_of: int32 [2, 15360, 1], P('scene', 'ctx'), may hold values from 0 to 95; in each aligned block of 160 rows (0 to 159, 160 to 319, ..., all dimensions but the last counted through in order) at most 4 rows name the same one
- cell_of: int32 [2, 15360], P('scene', 'ctx'), may hold values from 0 to 255
- bev_base: bfloat16 [2, 24576, 1024], P('scene', 'ctx'), may hold values from -3 to 3
- norm_gain: float32 [1024], replicated, may hold values from 0.1 to 1.9
- out_weight: bfloat16 [512, 1024], P('head'), may hold values from -0.25 to 0.25
- up_weight: bfloat16 [1024, 4096], P(None, 'head'), may hold values from -0.1875 to 0.1875
- down_weight: bfloat16 [4096, 1024], P('head'), may hold values from -0.09375 to 0.09375
Outputs:
- bev_out: bfloat16 [2, 24576, 1024], P('scene', ('ctx', 'head'))
The draws below stay inside these ranges and needn't reach their ends.
Inputs may be any that keep to these rules, and one draw needn't show every extreme that they name: `tile_of`: among the rows of one index of ctx no tile is named by more than 4 rows; on some devices a tile is named by exactly 4.
All inputs are finite; a program needn't handle non-finite values.
Results may differ from the reference program's by a relative error of at most 0.017.
Values may be sent and summed in bfloat16 or wider, within the bound.
No kernel may reach another device: no remote copies, remote signals or barrier semaphores. Data moves between devices by JAX's collectives and lax.ppermute only.
A program may use at most 32 MiB of HBM per device.

```python
import math
import jax
import jax.numpy as jnp
import numpy as np
from jax import lax

D = 1024
FF = 4096
HS = 64
HEADS = 8
TOK_DEV = 160
CELLS = 256
SCENES = 2
S = 15360
TILES = 96
HD = 512
CAP = 4


def aligned_parts(key):
    base_key = jax.random.fold_in(key, 41)
    fourth_key = jax.random.fold_in(base_key, 3)
    fifth_key = jax.random.fold_in(base_key, 4)
    key_rows = jax.random.permutation(fourth_key, S)[:9]
    sink_values = jnp.where(jax.random.bernoulli(fifth_key, 0.5, (SCENES, 1, HD)), 8.0, -8.0)
    return (key_rows, sink_values)


def draw_queries(key, part):
    main_key = jax.random.fold_in(key, 1)
    scale_key = jax.random.fold_in(key, 4)
    row_scale = jnp.exp(jax.random.uniform(scale_key, (SCENES, S, 1), jnp.float32, jnp.log(0.3), jnp.log(2.5)))
    drawn = jnp.clip(jax.random.normal(main_key, (SCENES, S, HD), jnp.float32) * row_scale, -8.0, 8.0)
    return drawn.astype(jnp.bfloat16)


def draw_key_states(key, part):
    main_key = jax.random.fold_in(key, 2)
    key_rows, sink_values = aligned_parts(key)
    drawn = jnp.clip(2.0 * jax.random.normal(main_key, (SCENES, S, HD), jnp.float32), -8.0, 8.0)
    drawn = drawn.at[:, key_rows[8:9], :].set(sink_values)
    return drawn.astype(jnp.bfloat16)


def touch_ends(values, key, least, largest):
    spot = [jax.random.randint(jax.random.fold_in(key, axis), (), 0, length) for axis, length in enumerate(values.shape)]
    main_axis = values.shape.index(max(values.shape))
    neighbour = spot[:main_axis] + [(spot[main_axis] + 1) % values.shape[main_axis]] + spot[main_axis + 1:]
    return values.at[tuple(spot)].set(least).at[tuple(neighbour)].set(largest)


def levels(own_key, extent, cuts, least, top_value):
    loudness, own = 1.0, jax.random.fold_in(own_key, 6)
    for position, shards_of in cuts:
        steps = jnp.exp(jax.random.uniform(jax.random.fold_in(own, position), (shards_of,), jnp.float32, least / len(cuts), top_value / len(cuts)))
        loudness = loudness * jnp.repeat(steps, extent[position] // shards_of).reshape([-1 if axis == position else 1 for axis in range(len(extent))])
    return loudness


def shared_out(key, own, number, rows, count, top, reach, lean):
    ranking = jax.random.permutation(key, count)
    packed, usual = load_shares(count, rows * top, reach, lean, True), load_shares(count, rows * top, reach, lean, False)
    places = jnp.arange(count)

    def named(sizes, turn):
        used = int((sizes > 0).sum())
        fixed = max(1, used // 4)
        moved = fixed + (places - fixed + turn * (used - fixed)) % max(1, count - fixed)
        return jnp.zeros((count,), jnp.int32).at[ranking[jnp.where(places < fixed, places, moved)]].set(jnp.asarray(sizes, jnp.int32))

    sizes = jnp.where(number % 4 == 0, named(packed, number // 4), named(usual, number - number // 4 - 1))
    mixed = jax.random.permutation(jax.random.fold_in(own, 3), count)
    giver, sink = mixed[0:count // 2 * 2:2], mixed[1:count // 2 * 2:2]
    margin = jnp.minimum(sizes[giver] - 1, reach - sizes[sink]) // 2
    margin = jnp.where((giver == ranking[0]) | (sink == ranking[0]) | (sizes[sink] == 0), 0, jnp.maximum(margin, 0))
    moved = jax.random.randint(jax.random.fold_in(own, 4), (count // 2,), 0, 1 << 20) % (margin + 1)
    sizes = sizes.at[giver].add(-moved).at[sink].add(moved)
    items = jnp.searchsorted(jnp.cumsum(sizes), jnp.arange(rows * top), side="right").astype(jnp.int32)
    grid = items.reshape(top, rows).T
    grid = grid[jax.random.permutation(jax.random.fold_in(own, 1), rows)]
    turn = jax.random.randint(jax.random.fold_in(own, 2), (rows, 1), 0, top)
    return jnp.take_along_axis(grid, (jnp.arange(top)[None, :] + turn) % top, axis=1)


def load_shares(amount, total, limit, slope, full):
    weights = [(1 << 20) // math.isqrt(rank ** slope) + 1 for rank in range(1, amount + 1)]
    largest = limit if full else min(limit, max(-(-total // amount), total * weights[0] // sum(weights)))
    least = 1 if total - largest >= amount - 1 else 0
    holding, surplus = [largest] + [least] * (amount - 1), total - largest - least * (amount - 1)
    while surplus > 0:
        free = [i for i in range(1, amount) if holding[i] < largest] or [i for i in range(1, amount) if holding[i] < limit]
        whole, budget = sum([weights[i] for i in free]), surplus
        for i in free:
            addition = min(limit - holding[i], max(1, budget * weights[i] // whole), surplus)
            holding[i] = holding[i] + addition
            surplus = surplus - addition
    return np.array(holding)


def scatter_about(own_key, extent, spread, limit, cuts=(), kind=jnp.bfloat16):
    factor_of = levels(own_key, extent, cuts, -0.22, 0.18) if cuts else 1.0
    values = jax.random.normal(own_key, extent, jnp.float32) * spread * factor_of
    return jnp.minimum(jnp.maximum(values, -limit), limit).astype(kind)


def setup_inputs(seed: int = 0) -> dict:
    seeds = jax.random.split(jax.random.key(seed), 12)
    queries = draw_queries(jax.random.fold_in(seeds[11], 71), 0)
    key_states = draw_key_states(jax.random.fold_in(seeds[11], 71), 0)
    value_states = scatter_about(seeds[2], (SCENES, S, HD), 1.0, 6.0, ((0, 2), (1, 96), (2, 4)))
    splat_weight = jnp.clip(jnp.exp(math.log(2.5) - 2.3025851 * jax.random.uniform(seeds[3], (SCENES, S), jnp.float32) ** levels(seeds[3], (SCENES, S), ((0, 2), (1, 96)), -0.2, 0.2)), 0.25, 2.5)
    tile_of_keys = jax.random.split(jax.random.fold_in(seeds[4], 1), SCENES * S // TOK_DEV)
    tile_of_turns = jax.random.permutation(jax.random.fold_in(seeds[4], 3), SCENES * S // TOK_DEV)
    tile_of = jax.vmap(lambda own, number: shared_out(jax.random.fold_in(seeds[4], 2), own, number, TOK_DEV, TILES, 1, CAP, 2))(tile_of_keys, tile_of_turns).reshape((SCENES, S, 1))
    cell_of = touch_ends(jax.random.randint(seeds[5], (SCENES, S), 0, CELLS), jax.random.fold_in(seeds[5], 1), 0, CELLS - 1).astype(jnp.int32)
    bev_base = scatter_about(seeds[6], (SCENES, TILES * CELLS, D), 0.5, 3.0, ((0, 2), (1, 96)))
    norm_gain = jnp.clip(1.0 + 0.18 * jax.random.normal(seeds[7], (D,), jnp.float32), 0.1, 1.9)
    out_weight = scatter_about(seeds[8], (HD, D), HD ** -0.5, 0.25, ((0, 4),))
    up_weight = scatter_about(seeds[9], (D, FF), D ** -0.5, 0.1875, ((1, 4),))
    down_weight = scatter_about(seeds[10], (FF, D), FF ** -0.5, 0.09375, ((0, 4),))
    return {"queries": queries, "key_states": key_states, "value_states": value_states, "splat_weight": splat_weight, "tile_of": tile_of, "cell_of": cell_of, "bev_base": bev_base, "norm_gain": norm_gain, "out_weight": out_weight, "up_weight": up_weight, "down_weight": down_weight}


def attend_scene(query_rows, key_rows, value_rows):
    total = query_rows.shape[0]
    head_scale = 1.0 / math.sqrt(HS)
    block = math.gcd(total, 512)
    query_blocks = query_rows.reshape(total // block, block, HEADS, HS)
    key_heads = key_rows.astype(jnp.float32).reshape(total, HEADS, HS)
    value_heads = value_rows.astype(jnp.float32).reshape(total, HEADS, HS)

    def one_block(query_block):
        scores = jnp.einsum('qhd,khd->hqk', query_block.astype(jnp.float32), key_heads) * head_scale
        row_max = lax.optimization_barrier(jnp.max(scores, axis=2, keepdims=True))
        exp_scores = jnp.exp(scores - row_max)
        denominator = lax.optimization_barrier(jnp.sum(exp_scores, axis=2))
        probs = lax.optimization_barrier(exp_scores.astype(jnp.bfloat16))
        numerator = jnp.einsum('hqk,khd->qhd', probs.astype(jnp.float32), value_heads)
        return numerator / jnp.transpose(denominator)[:, :, None]
    attended = lax.map(one_block, query_blocks)
    return attended.reshape(total, HEADS * HS)

def reference(queries, key_states, value_states, splat_weight, tile_of, cell_of, bev_base, norm_gain, out_weight, up_weight, down_weight):
    outputs = []
    for scene_index in range(SCENES):
        attended = attend_scene(queries[scene_index], key_states[scene_index], value_states[scene_index])
        weighted = lax.optimization_barrier((attended * splat_weight[scene_index][:, None]).astype(jnp.bfloat16))
        target = (tile_of[scene_index, :, 0] * CELLS + cell_of[scene_index]).astype(jnp.int32)
        cell_features = jax.ops.segment_sum(weighted.astype(jnp.float32), target, num_segments=TILES * CELLS).astype(jnp.bfloat16)
        projected = jnp.dot(cell_features, out_weight, preferred_element_type=jnp.float32)
        bev = bev_base[scene_index].astype(jnp.float32) + projected
        mean_square = lax.optimization_barrier(jnp.mean(bev * bev, axis=1, keepdims=True))
        normed = (bev * lax.rsqrt(mean_square + 1e-06) * norm_gain[None, :]).astype(jnp.bfloat16)
        hidden = jax.nn.gelu(jnp.dot(normed, up_weight, preferred_element_type=jnp.float32), approximate=False).astype(jnp.bfloat16)
        mixed = jnp.dot(hidden, down_weight, preferred_element_type=jnp.float32)
        outputs.append((bev + mixed).astype(jnp.bfloat16))
    return jnp.stack(outputs)
```

```python
import functools
import math

import jax
import jax.numpy as jnp
from jax import lax
from jax.experimental import pallas as pl
from jax.experimental.pallas import tpu as pltpu
from jax.sharding import Mesh
from jax.sharding import PartitionSpec as P

HS = 64
LANES = 128
SLOTS = 4
PIECE = 20
EXPONENT = math.log2(math.e) / math.sqrt(HS)
VMEM_LIMIT = 56 * 1024 * 1024

f32 = jnp.float32
bf16 = jnp.bfloat16


def dot(a, b):
    return lax.dot_general(a, b, (((1,), (0,)), ((), ())), preferred_element_type=f32)


def dot_nt(a, b):
    return lax.dot_general(a, b, (((1,), (1,)), ((), ())), preferred_element_type=f32)


def attend_kernel(tiles, own_ref, other_ref, q_ref, out_ref, k_s, v_s, ox_s, slot_s, slot_t):
    blocks, tok = own_ref.shape[0], own_ref.shape[1] // 2
    span = blocks * tok
    groups = q_ref.shape[0]
    low = lax.broadcasted_iota(jnp.int32, (1, LANES), 1) < HS
    low_f = jnp.where(low, 1.0, 0.0)
    low_b, high_b = low_f.astype(bf16), (1.0 - low_f).astype(bf16)
    for part, kv_ref in enumerate((own_ref, other_ref)):
        rows = pl.ds(part * span, span)
        k_s[rows, :] = kv_ref[:, :tok, :].reshape(span, LANES)
        values = kv_ref[:, tok:, :].reshape(span, LANES)
        v_s[0, rows, :] = values * low_b + high_b
        v_s[1, rows, :] = values * high_b + low_b
    lane = lax.broadcasted_iota(jnp.int32, (tok, LANES), 1)
    lane_f = lane.astype(f32)
    for group in range(groups):
        q = q_ref[group, :, :LANES]
        meta = q_ref[group, :, LANES:].astype(f32)
        tile, cell = meta[:, 0:1], meta[:, 2:3]
        place = meta[:, 1:2] + float(group * SLOTS)
        splat = meta[:, 3:4] + meta[:, 4:5]
        rows = pl.ds(group * tok, tok)
        sums = []
        extra = jnp.where(lane_f == 96.0 + place, cell, 0.0)
        for head, keep in enumerate((low_b, high_b)):
            s = dot_nt(q * keep, k_s[...])
            top = jnp.max(s, axis=1, keepdims=True)
            p = jnp.exp2((s - top) * EXPONENT).astype(bf16)
            o = dot(p, v_s[head])
            at = LANES - 1 if head == 0 else 0
            total = o[:, at : at + 1]
            sums.append(o * (splat / total))
            left = top * EXPONENT + jnp.log2(total)
            for step in range(3):
                piece = left.astype(bf16).astype(f32)
                left = left - piece
                extra = jnp.where(lane_f == step * 32.0 + head * 16.0 + place, piece, extra)
        ox_s[rows, :] = jnp.where(low, sums[0], sums[1]).astype(bf16)
        ox_s[pl.ds(groups * tok + group * tok, tok), :] = extra.astype(bf16)
        slot_s[rows, :] = jnp.where(
            lane == 0, tile * PIECE + place, jnp.where(lane == 1, tile * PIECE + float(SLOTS * groups), -1.0)
        )
    slot_t[...] = jnp.transpose(slot_s[...])
    chunk = 8 * PIECE * 3
    width = groups * tok
    for begin in range(0, tiles * PIECE, chunk):
        row = (lax.broadcasted_iota(jnp.int32, (chunk, width), 0) + begin).astype(f32)
        main = jnp.where(row == slot_t[0:1, :], 1.0, 0.0).astype(bf16)
        tail = jnp.where(row == slot_t[1:2, :], 1.0, 0.0).astype(bf16)
        packed = dot(main, ox_s[:width, :]) + dot(tail, ox_s[width:, :])
        out_ref[pl.ds(begin, chunk), :] = packed.astype(bf16)


def attend(own, other, q_all, tiles):
    blocks, tok2, _ = own.shape
    groups, tok, _ = q_all.shape
    keys = blocks * tok2
    return pl.pallas_call(
        functools.partial(attend_kernel, tiles),
        out_shape=jax.ShapeDtypeStruct((tiles * PIECE, LANES), bf16),
        in_specs=[pl.BlockSpec(memory_space=pltpu.VMEM)] * 3,
        out_specs=pl.BlockSpec(memory_space=pltpu.VMEM),
        scratch_shapes=[
            pltpu.VMEM((keys, LANES), bf16),
            pltpu.VMEM((2, keys, LANES), bf16),
            pltpu.VMEM((2 * groups * tok, LANES), bf16),
            pltpu.VMEM((groups * tok, LANES), f32),
            pltpu.VMEM((LANES, groups * tok), f32),
        ],
        compiler_params=pltpu.CompilerParams(vmem_limit_bytes=VMEM_LIMIT),
        name="attend_pack",
    )(own, other, q_all)


def splat_kernel(cells, groups, x_ref, out_ref, x_s, y_s, r_s):
    sources = x_ref.shape[0] // PIECE
    slots = groups * SLOTS
    x_s[...] = x_ref[...].astype(f32)
    meta = x_s[pl.ds(slots, sources, stride=PIECE), :]
    lse = meta + pltpu.roll(meta, LANES - 32, 1) + pltpu.roll(meta, LANES - 64, 1)
    lse = lse.reshape(sources // (2 * groups), 2 * groups, LANES)
    turns = [lse] + [pltpu.roll(lse, 2 * k, 1) for k in range(1, groups)]
    top = functools.reduce(jnp.maximum, turns)
    powers = [jnp.exp2(t - top) for t in turns]
    weight = powers[0] / functools.reduce(jnp.add, powers)
    weight = weight.reshape(sources, LANES)
    lane = lax.broadcasted_iota(jnp.int32, (sources, LANES), 1)
    y_s[...] = jnp.zeros_like(y_s)
    y_s[:sources, :] = jnp.where(lane < 32, weight, meta)
    y_t = jnp.transpose(y_s[...])
    r_s[...] = jnp.zeros_like(r_s)
    for slot in range(slots):
        r_s[pl.ds(slot * LANES, sources), :] = x_s[pl.ds(slot, sources, stride=PIECE), :].astype(bf16)
    cell = (lax.broadcasted_iota(jnp.int32, (cells, LANES), 0) + 1).astype(f32)
    hits = [cell == y_t[96 + slot : 97 + slot, :] for slot in range(slots)]
    sums = []
    for head in range(2):
        spread = jnp.concatenate(
            [
                jnp.where(hits[slot], y_t[head * 16 + slot : head * 16 + slot + 1, :], 0.0).astype(bf16)
                for slot in range(slots)
            ],
            axis=1,
        )
        sums.append(dot(spread, r_s[...]))
    low = lax.broadcasted_iota(jnp.int32, (1, LANES), 1) < HS
    out_ref[...] = jnp.where(low, sums[0], sums[1]).astype(bf16)


def splat(received, cells, groups):
    rows = received.shape[0]
    return pl.pallas_call(
        functools.partial(splat_kernel, cells, groups),
        out_shape=jax.ShapeDtypeStruct((cells, LANES), bf16),
        in_specs=[pl.BlockSpec(memory_space=pltpu.VMEM)],
        out_specs=pl.BlockSpec(memory_space=pltpu.VMEM),
        scratch_shapes=[
            pltpu.VMEM((rows, LANES), f32),
            pltpu.VMEM((LANES, LANES), f32),
            pltpu.VMEM((groups * SLOTS * LANES, LANES), bf16),
        ],
        compiler_params=pltpu.CompilerParams(vmem_limit_bytes=VMEM_LIMIT),
        name="join_splat",
    )(received)


def mlp_kernel(own_ref, f_ref, ow_ref, base_ref, gain_ref, up_ref, down_ref, bev_ref, mix_ref, bev_s):
    heads = f_ref.shape[0]
    share = bev_ref.shape[0]
    bev = base_ref[...].astype(f32) + functools.reduce(
        jnp.add, [dot(f_ref[h], ow_ref[h]) for h in range(heads)]
    )
    bev_s[...] = bev
    mean_square = jnp.mean(bev * bev, axis=1, keepdims=True)
    normed = (bev * lax.rsqrt(mean_square + 1e-06) * gain_ref[...]).astype(bf16)
    hidden_units = up_ref.shape[1]
    step = 256
    mixed = None
    for begin in range(0, hidden_units, step):
        u = dot(normed, up_ref[:, begin : begin + step])
        hidden = (0.5 * u * (1.0 + lax.erf(u * math.sqrt(0.5)))).astype(bf16)
        term = dot(hidden, down_ref[begin : begin + step, :])
        mixed = term if mixed is None else mixed + term
    mix_ref[...] = mixed.astype(bf16)
    start = pl.multiple_of(own_ref[0] * share, share)
    bev_ref[...] = bev_s[pl.ds(start, share), :]


def mlp(own, features, out_weight, base, gain, up, down):
    heads = features.shape[0]
    cells, width = base.shape
    vmem = pl.BlockSpec(memory_space=pltpu.VMEM)
    return pl.pallas_call(
        mlp_kernel,
        out_shape=(
            jax.ShapeDtypeStruct((cells // heads, width), f32),
            jax.ShapeDtypeStruct((cells, width), bf16),
        ),
        in_specs=[pl.BlockSpec(memory_space=pltpu.SMEM)] + [vmem] * 6,
        out_specs=(vmem, vmem),
        scratch_shapes=[pltpu.VMEM((cells, width), f32)],
        compiler_params=pltpu.CompilerParams(vmem_limit_bytes=VMEM_LIMIT),
        name="project_mlp",
    )(own, features, out_weight, base, gain, up, down)


def to_all(x, axis):
    count = lax.axis_size(axis)
    return lax.all_to_all(jnp.broadcast_to(x[None], (count,) + x.shape), axis, 0, 0)


def body(
    queries,
    key_states,
    value_states,
    splat_weight,
    tile_of,
    cell_of,
    bev_base,
    norm_gain,
    out_weight,
    up_weight,
    down_weight,
):
    tok = queries.shape[1]
    tiles = lax.axis_size("z") * lax.axis_size("y") * lax.axis_size("core")
    groups = lax.axis_size("y")
    heads = lax.axis_size("head")
    cells = bev_base.shape[1]
    tile = tile_of[0, :, 0]
    index = jnp.arange(tok, dtype=jnp.int32)
    earlier = (tile[:, None] == tile[None, :]) & (index[None, :] < index[:, None])
    rank = jnp.sum(earlier.astype(jnp.int32), axis=1)
    coarse = lax.reduce_precision(splat_weight[0], 8, 7)
    fine = splat_weight[0] - coarse
    columns = [tile.astype(f32), rank.astype(f32), (cell_of[0] + 1).astype(f32), coarse, fine]
    meta = jnp.pad(jnp.stack(columns, axis=1), ((0, 0), (0, LANES - len(columns)))).astype(bf16)
    q_all = to_all(jnp.concatenate([queries[0], meta], axis=1), "y")
    ow_all = to_all(out_weight, "head")
    kv = jnp.concatenate([key_states[0], value_states[0]], axis=0)
    own_kv = lax.all_gather(kv, "z")
    other_kv = lax.ppermute(own_kv, "core", [(0, 1), (1, 0)])
    packed = attend(own_kv, other_kv, q_all, tiles)
    received = lax.all_to_all(packed.reshape(tiles, PIECE, LANES), ("z", "y", "core"), 0, 0)
    features = splat(received.reshape(tiles * PIECE, LANES), cells, groups)
    features = to_all(features, "head")
    own = lax.axis_index("head").astype(jnp.int32).reshape(1)
    bev_rows, mixed = mlp(own, features, ow_all, bev_base[0], norm_gain[None, :], up_weight, down_weight)
    mixed = lax.all_to_all(mixed.reshape(heads, cells // heads, mixed.shape[1]), "head", 0, 0)
    return (bev_rows + jnp.sum(mixed.astype(f32), axis=0)).astype(bf16)[None]


def solution(mesh):
    core, y = 2, 4
    z = mesh.shape["ctx"] // (core * y)
    split = Mesh(
        mesh.devices.reshape(z, y, core, mesh.shape["head"], mesh.shape["scene"]),
        ("z", "y", "core", "head", "scene"),
    )
    ctx = ("z", "y", "core")
    placed = (
        P("scene", ctx, "head"),
        P("scene", ctx, "head"),
        P("scene", ctx, "head"),
        P("scene", ctx),
        P("scene", ctx, None),
        P("scene", ctx),
        P("scene", ctx, None),
        P(),
        P("head", None),
        P(None, "head"),
        P("head", None),
    )
    return jax.shard_map(
        body,
        mesh=split,
        in_specs=placed,
        out_specs=P("scene", ctx + ("head",), None),
        check_vma=False,
    )
```

```python
import functools
import math

import jax
import jax.numpy as jnp
from jax import lax
from jax.experimental import pallas as pl
from jax.experimental.pallas import tpu as pltpu
from jax.sharding import Mesh
from jax.sharding import PartitionSpec as P

HS = 64
LANES = 128
SLOTS = 4
PIECE = 24
EXPONENT = math.log2(math.e) / math.sqrt(HS)
MIB = 1024 * 1024

f32 = jnp.float32
bf16 = jnp.bfloat16


def dot(a, b):
    return lax.dot_general(a, b, (((1,), (0,)), ((), ())), preferred_element_type=f32)


def dot_nt(a, b):
    return lax.dot_general(a, b, (((1,), (1,)), ((), ())), preferred_element_type=f32)


def prologue_kernel(q_ref, k_ref, v_ref, tile_ref, cell_ref, splat_ref, q_out, kv_out, rows_s):
    copies, tok = q_out.shape[0], q_out.shape[1]
    tile = tile_ref[...].astype(f32)
    coarse = splat_ref[...].astype(bf16).astype(f32)
    rows_s[...] = jnp.zeros_like(rows_s)
    rows_s[0:1, :tok] = tile
    rows_s[2:3, :tok] = (cell_ref[...] + 1).astype(f32)
    rows_s[3:4, :tok] = coarse
    rows_s[4:5, :tok] = splat_ref[...] - coarse
    columns = jnp.transpose(rows_s[...])[:tok, :]
    shape = (tok, tok)
    earlier = lax.broadcasted_iota(jnp.int32, shape, 1) < lax.broadcasted_iota(jnp.int32, shape, 0)
    alike = jnp.where(columns[:, 0:1] == tile, 1.0, 0.0)
    rank = jnp.sum(jnp.where(earlier, alike, 0.0), axis=1, keepdims=True)
    lane = lax.broadcasted_iota(jnp.int32, (tok, LANES), 1)
    meta = jnp.where(lane == 1, rank, columns).astype(bf16)
    for copy in range(copies):
        q_out[copy, :, :LANES] = q_ref[0]
        q_out[copy, :, LANES:] = meta
    kv_out[:tok, :] = k_ref[0]
    kv_out[tok:, :] = v_ref[0]


def prologue(queries, key_states, value_states, tile, cell, splat_weight, copies):
    tok = queries.shape[1]
    vmem = pl.BlockSpec(memory_space=pltpu.VMEM)
    return pl.pallas_call(
        prologue_kernel,
        out_shape=(
            jax.ShapeDtypeStruct((copies, tok, 2 * LANES), bf16),
            jax.ShapeDtypeStruct((2 * tok, LANES), bf16),
        ),
        in_specs=[vmem] * 6,
        out_specs=(vmem, vmem),
        scratch_shapes=[pltpu.VMEM((LANES, 2 * LANES), f32)],
        compiler_params=pltpu.CompilerParams(vmem_limit_bytes=58 * MIB),
        name="prologue",
    )(queries, key_states, value_states, tile, cell, splat_weight)


def attend_block(q_ref, group, k_s, v_s):
    low = lax.broadcasted_iota(jnp.int32, (1, LANES), 1) < HS
    q = q_ref[group, :, :LANES]
    for head in range(2):
        keep = jnp.where(low if head == 0 else ~low, 1.0, 0.0).astype(bf16)
        s = dot_nt(q * keep, k_s[...])
        top = jnp.max(s, axis=1, keepdims=True)
        p = jnp.exp2((s - top) * EXPONENT).astype(bf16)
        yield head, top * EXPONENT, dot(p, v_s[head])


def stage_keys(kv_ref, k_s, v_s):
    blocks, tok = kv_ref.shape[0], kv_ref.shape[1] // 2
    span = blocks * tok
    low = jnp.where(lax.broadcasted_iota(jnp.int32, (1, LANES), 1) < HS, 1.0, 0.0)
    low_b, high_b = low.astype(bf16), (1.0 - low).astype(bf16)
    k_s[...] = kv_ref[:, :tok, :].reshape(span, LANES)
    values = kv_ref[:, tok:, :].reshape(span, LANES)
    v_s[0] = values * low_b + high_b
    v_s[1] = values * high_b + low_b


def first_kernel(kv_ref, q_ref, top_ref, sum_ref, k_s, v_s):
    groups, tok = q_ref.shape[0], q_ref.shape[1]
    stage_keys(kv_ref, k_s, v_s)
    for group in range(groups):
        rows = pl.ds(group * tok, tok)
        for head, top, sums in attend_block(q_ref, group, k_s, v_s):
            top_ref[head, rows, :] = jnp.broadcast_to(top, (tok, LANES))
            sum_ref[head, rows, :] = sums


def second_kernel(tiles, kv_ref, q_ref, top_ref, sum_ref, _, out_ref, k_s, v_s, ox_s, slot_s, slot_t):
    groups, tok = q_ref.shape[0], q_ref.shape[1]
    stage_keys(kv_ref, k_s, v_s)
    low = lax.broadcasted_iota(jnp.int32, (1, LANES), 1) < HS
    lane = lax.broadcasted_iota(jnp.int32, (tok, LANES), 1)
    lane_f = lane.astype(f32)
    width = groups * tok
    for group in range(groups):
        meta = q_ref[group, :, LANES:].astype(f32)
        tile, cell = meta[:, 0:1], meta[:, 2:3]
        place = meta[:, 1:2] + float(group * SLOTS)
        gain = meta[:, 3:4] + meta[:, 4:5]
        rows = pl.ds(group * tok, tok)
        sums = []
        extra = jnp.where(lane_f == 96.0 + place, cell, 0.0)
        for head, top_b, sum_b in attend_block(q_ref, group, k_s, v_s):
            top_a = top_ref[head, rows, :][:, 0:1]
            top = jnp.maximum(top_a, top_b)
            o = sum_ref[head, rows, :] * jnp.exp2(top_a - top) + sum_b * jnp.exp2(top_b - top)
            at = LANES - 1 if head == 0 else 0
            total = o[:, at : at + 1]
            sums.append(o * (gain / total))
            left = top + jnp.log2(total)
            for step in range(3):
                piece = left.astype(bf16).astype(f32)
                left = left - piece
                extra = jnp.where(lane_f == step * 32.0 + head * 16.0 + place, piece, extra)
        ox_s[rows, :] = jnp.where(low, sums[0], sums[1]).astype(bf16)
        ox_s[pl.ds(width + group * tok, tok), :] = extra.astype(bf16)
        slot_s[rows, :] = jnp.where(
            lane == 0, tile * PIECE + place, jnp.where(lane == 1, tile * PIECE + float(SLOTS * groups), -1.0)
        )
    slot_t[...] = jnp.transpose(slot_s[...])
    chunk = 16 * PIECE
    for begin in range(0, tiles * PIECE, chunk):
        row = (lax.broadcasted_iota(jnp.int32, (chunk, width), 0) + begin).astype(f32)
        main = jnp.where(row == slot_t[0:1, :], 1.0, 0.0).astype(bf16)
        tail = jnp.where(row == slot_t[1:2, :], 1.0, 0.0).astype(bf16)
        packed = dot(main, ox_s[:width, :]) + dot(tail, ox_s[width:, :])
        out_ref[pl.ds(begin, chunk), :] = packed.astype(bf16)


def attention_cost(queries, keys):
    return pl.CostEstimate(
        flops=2 * 2 * 2 * queries * keys * LANES, bytes_accessed=4 * queries * LANES, transcendentals=2 * queries * keys
    )


def attend_first(kv, q_all):
    blocks, tok2, _ = kv.shape
    groups, tok, _ = q_all.shape
    span, rows = blocks * tok2 // 2, groups * tok
    vmem = pl.BlockSpec(memory_space=pltpu.VMEM)
    state = jax.ShapeDtypeStruct((2, rows, LANES), f32)
    return pl.pallas_call(
        first_kernel,
        out_shape=(state, state),
        in_specs=[vmem, vmem],
        out_specs=(vmem, vmem),
        scratch_shapes=[pltpu.VMEM((span, LANES), bf16), pltpu.VMEM((2, span, LANES), bf16)],
        compiler_params=pltpu.CompilerParams(vmem_limit_bytes=20 * MIB),
        cost_estimate=attention_cost(rows, span),
        name="attend_own_core",
    )(kv, q_all)


def attend_second(kv, q_all, top, sums, early, tiles):
    blocks, tok2, _ = kv.shape
    groups, tok, _ = q_all.shape
    span, rows = blocks * tok2 // 2, groups * tok
    vmem = pl.BlockSpec(memory_space=pltpu.VMEM)
    return pl.pallas_call(
        functools.partial(second_kernel, tiles),
        out_shape=jax.ShapeDtypeStruct((tiles * PIECE, LANES), bf16),
        in_specs=[vmem] * 4 + [pl.BlockSpec(memory_space=pl.ANY)],
        out_specs=vmem,
        scratch_shapes=[
            pltpu.VMEM((span, LANES), bf16),
            pltpu.VMEM((2, span, LANES), bf16),
            pltpu.VMEM((2 * rows, LANES), bf16),
            pltpu.VMEM((rows, LANES), f32),
            pltpu.VMEM((LANES, rows), f32),
        ],
        compiler_params=pltpu.CompilerParams(vmem_limit_bytes=24 * MIB),
        cost_estimate=attention_cost(rows, span),
        name="attend_other_core",
    )(kv, q_all, top, sums, early)


def splat_kernel(cells, groups, x_ref, out_ref, x_s, y_s, r_s):
    sources = x_ref.shape[0] // PIECE
    slots = groups * SLOTS
    x_s[...] = x_ref[...].astype(f32)
    meta = x_s[pl.ds(slots, sources, stride=PIECE), :]
    lse = meta + pltpu.roll(meta, LANES - 32, 1) + pltpu.roll(meta, LANES - 64, 1)
    lse = lse.reshape(sources // (2 * groups), 2 * groups, LANES)
    turns = [lse] + [pltpu.roll(lse, 2 * k, 1) for k in range(1, groups)]
    top = functools.reduce(jnp.maximum, turns)
    powers = [jnp.exp2(t - top) for t in turns]
    weight = powers[0] / functools.reduce(jnp.add, powers)
    weight = weight.reshape(sources, LANES)
    lane = lax.broadcasted_iota(jnp.int32, (sources, LANES), 1)
    y_s[...] = jnp.zeros_like(y_s)
    y_s[:sources, :] = jnp.where(lane < 32, weight, meta)
    y_t = jnp.transpose(y_s[...])
    r_s[...] = jnp.zeros_like(r_s)
    for slot in range(slots):
        r_s[pl.ds(slot * LANES, sources), :] = x_s[pl.ds(slot, sources, stride=PIECE), :].astype(bf16)
    cell = (lax.broadcasted_iota(jnp.int32, (cells, LANES), 0) + 1).astype(f32)
    hits = [cell == y_t[96 + slot : 97 + slot, :] for slot in range(slots)]
    sums = []
    for head in range(2):
        spread = jnp.concatenate(
            [
                jnp.where(hits[slot], y_t[head * 16 + slot : head * 16 + slot + 1, :], 0.0).astype(bf16)
                for slot in range(slots)
            ],
            axis=1,
        )
        sums.append(dot(spread, r_s[...]))
    low = lax.broadcasted_iota(jnp.int32, (1, LANES), 1) < HS
    features = jnp.where(low, sums[0], sums[1]).astype(bf16)
    for copy in range(out_ref.shape[0]):
        out_ref[copy] = features


def splat(received, cells, groups, copies):
    rows = received.shape[0]
    return pl.pallas_call(
        functools.partial(splat_kernel, cells, groups),
        out_shape=jax.ShapeDtypeStruct((copies, cells, LANES), bf16),
        in_specs=[pl.BlockSpec(memory_space=pltpu.VMEM)],
        out_specs=pl.BlockSpec(memory_space=pltpu.VMEM),
        scratch_shapes=[
            pltpu.VMEM((rows, LANES), f32),
            pltpu.VMEM((LANES, LANES), f32),
            pltpu.VMEM((groups * SLOTS * LANES, LANES), bf16),
        ],
        compiler_params=pltpu.CompilerParams(vmem_limit_bytes=12 * MIB),
        name="join_splat",
    )(received)


def mlp_kernel(own_ref, f_ref, ow_ref, base_ref, gain_ref, up_ref, down_ref, bev_ref, mix_ref, bev_s):
    heads = f_ref.shape[0]
    share = bev_ref.shape[0]
    features = jnp.concatenate([f_ref[h] for h in range(heads)], axis=1)
    bev = base_ref[...].astype(f32) + dot(features, ow_ref[...].reshape(features.shape[1], -1))
    bev_s[...] = bev
    mean_square = jnp.mean(bev * bev, axis=1, keepdims=True)
    normed = (bev * lax.rsqrt(mean_square + 1e-06) * gain_ref[...]).astype(bf16)
    hidden_units = up_ref.shape[1]
    step = 256
    mixed = None
    for begin in range(0, hidden_units, step):
        u = dot(normed, up_ref[:, begin : begin + step])
        hidden = (0.5 * u * (1.0 + lax.erf(u * math.sqrt(0.5)))).astype(bf16)
        term = dot(hidden, down_ref[begin : begin + step, :])
        mixed = term if mixed is None else mixed + term
    mix_ref[...] = mixed.astype(bf16)
    start = pl.multiple_of(own_ref[0] * share, share)
    bev_ref[...] = bev_s[pl.ds(start, share), :]


def mlp(own, features, out_weight, base, gain, up, down):
    heads = features.shape[0]
    cells, width = base.shape
    vmem = pl.BlockSpec(memory_space=pltpu.VMEM)
    return pl.pallas_call(
        mlp_kernel,
        out_shape=(
            jax.ShapeDtypeStruct((cells // heads, width), f32),
            jax.ShapeDtypeStruct((cells, width), bf16),
        ),
        in_specs=[pl.BlockSpec(memory_space=pltpu.SMEM)] + [vmem] * 6,
        out_specs=(vmem, vmem),
        scratch_shapes=[pltpu.VMEM((cells, width), f32)],
        compiler_params=pltpu.CompilerParams(vmem_limit_bytes=20 * MIB),
        name="project_mlp",
    )(own, features, out_weight, base, gain, up, down)


def to_all(x, axis):
    count = lax.axis_size(axis)
    return lax.all_to_all(jnp.broadcast_to(x[None], (count,) + x.shape), axis, 0, 0)


def body(
    queries,
    key_states,
    value_states,
    splat_weight,
    tile_of,
    cell_of,
    bev_base,
    norm_gain,
    out_weight,
    up_weight,
    down_weight,
):
    tok = queries.shape[1]
    tiles = lax.axis_size("z") * lax.axis_size("y") * lax.axis_size("core")
    groups = lax.axis_size("y")
    heads = lax.axis_size("head")
    cells = bev_base.shape[1]
    q_copies, kv = prologue(
        queries, key_states, value_states, tile_of.reshape(1, tok), cell_of, splat_weight, groups
    )
    q_all = lax.all_to_all(q_copies, "y", 0, 0)
    ow_all = to_all(out_weight, "head")
    own_kv = lax.all_gather(kv, "z")
    other_kv = lax.ppermute(own_kv, "core", [(0, 1), (1, 0)])
    top, sums = attend_first(own_kv, q_all)
    packed = attend_second(other_kv, q_all, top, sums, ow_all, tiles)
    received = lax.all_to_all(packed.reshape(tiles, PIECE, LANES), ("z", "y", "core"), 0, 0)
    features = splat(received.reshape(tiles * PIECE, LANES), cells, groups, heads)
    features = lax.all_to_all(features, "head", 0, 0)
    own = lax.axis_index("head").astype(jnp.int32).reshape(1)
    bev_rows, mixed = mlp(own, features, ow_all, bev_base[0], norm_gain[None, :], up_weight, down_weight)
    mixed = lax.all_to_all(mixed.reshape(heads, cells // heads, mixed.shape[1]), "head", 0, 0)
    return (bev_rows + jnp.sum(mixed.astype(f32), axis=0)).astype(bf16)[None]


def solution(mesh):
    core, y = 2, 4
    z = mesh.shape["ctx"] // (core * y)
    split = Mesh(
        mesh.devices.reshape(z, y, core, mesh.shape["head"], mesh.shape["scene"]),
        ("z", "y", "core", "head", "scene"),
    )
    ctx = ("z", "y", "core")
    placed = (
        P("scene", ctx, "head"),
        P("scene", ctx, "head"),
        P("scene", ctx, "head"),
        P("scene", ctx),
        P("scene", ctx, None),
        P("scene", ctx),
        P("scene", ctx, None),
        P(),
        P("head", None),
        P(None, "head"),
        P("head", None),
    )
    return jax.shard_map(
        body,
        mesh=split,
        in_specs=placed,
        out_specs=P("scene", ctx + ("head",), None),
        check_vma=False,
    )
```

```python
import functools
import math

import jax
import jax.numpy as jnp
from jax import lax
from jax.experimental import pallas as pl
from jax.experimental.pallas import tpu as pltpu
from jax.sharding import Mesh
from jax.sharding import PartitionSpec as P

HS = 64
LANES = 128
SLOTS = 4
PIECE = 8
EXTRA = 16
EXPONENT = math.log2(math.e) / math.sqrt(HS)
MIB = 1024 * 1024

f32 = jnp.float32
bf16 = jnp.bfloat16


def dot(a, b):
    return lax.dot_general(a, b, (((1,), (0,)), ((), ())), preferred_element_type=f32)


def dot_nt(a, b):
    return lax.dot_general(a, b, (((1,), (1,)), ((), ())), preferred_element_type=f32)


def prologue_kernel(q_ref, k_ref, v_ref, q_out, kv_out):
    tok = q_ref.shape[1]
    for copy in range(q_out.shape[0]):
        q_out[copy] = q_ref[0]
    kv_out[:tok, :] = k_ref[0]
    kv_out[tok:, :] = v_ref[0]


def prologue(queries, key_states, value_states, copies):
    tok = queries.shape[1]
    vmem = pl.BlockSpec(memory_space=pltpu.VMEM)
    return pl.pallas_call(
        prologue_kernel,
        out_shape=(
            jax.ShapeDtypeStruct((copies, tok, LANES), bf16),
            jax.ShapeDtypeStruct((2 * tok, LANES), bf16),
        ),
        in_specs=[vmem] * 3,
        out_specs=(vmem, vmem),
        compiler_params=pltpu.CompilerParams(vmem_limit_bytes=58 * MIB),
        name="prologue",
    )(queries, key_states, value_states)


def attend_block(q_ref, group, k_s, v_s):
    low = lax.broadcasted_iota(jnp.int32, (1, LANES), 1) < HS
    q = q_ref[group]
    for head in range(2):
        keep = jnp.where(low if head == 0 else ~low, 1.0, 0.0).astype(bf16)
        s = dot_nt(q * keep, k_s[...])
        top = jnp.max(s, axis=1, keepdims=True)
        p = jnp.exp2((s - top) * EXPONENT).astype(bf16)
        yield head, top * EXPONENT, dot(p, v_s[head])


def stage_keys(kv_ref, k_s, v_s):
    blocks, tok = kv_ref.shape[0], kv_ref.shape[1] // 2
    span = blocks * tok
    low = jnp.where(lax.broadcasted_iota(jnp.int32, (1, LANES), 1) < HS, 1.0, 0.0)
    low_b, high_b = low.astype(bf16), (1.0 - low).astype(bf16)
    k_s[...] = kv_ref[:, :tok, :].reshape(span, LANES)
    values = kv_ref[:, tok:, :].reshape(span, LANES)
    v_s[0] = values * low_b + high_b
    v_s[1] = values * high_b + low_b


def other_half(head):
    return (LANES - 1, LANES - 2) if head == 0 else (0, 1)


def first_kernel(kv_ref, q_ref, sum_ref, k_s, v_s):
    groups, tok = q_ref.shape[0], q_ref.shape[1]
    stage_keys(kv_ref, k_s, v_s)
    lane = lax.broadcasted_iota(jnp.int32, (1, LANES), 1)
    for group in range(groups):
        for head, top, sums in attend_block(q_ref, group, k_s, v_s):
            sum_ref[head, pl.ds(group * tok, tok), :] = jnp.where(lane == other_half(head)[1], top, sums)


def second_kernel(kv_ref, q_ref, sum_ref, out_ref, k_s, v_s, lse_s):
    groups, tok = q_ref.shape[0], q_ref.shape[1]
    padded = lse_s.shape[0] // groups
    stage_keys(kv_ref, k_s, v_s)
    lane = lax.broadcasted_iota(jnp.int32, (tok, LANES), 1)
    lse_s[...] = jnp.zeros_like(lse_s)
    for group in range(groups):
        sums = []
        extra = jnp.zeros((tok, LANES), f32)
        for head, top_b, sum_b in attend_block(q_ref, group, k_s, v_s):
            at, top_at = other_half(head)
            sum_a = sum_ref[head, pl.ds(group * tok, tok), :]
            top_a = sum_a[:, top_at : top_at + 1]
            top = jnp.maximum(top_a, top_b)
            o = sum_a * jnp.exp2(top_a - top) + sum_b * jnp.exp2(top_b - top)
            total = o[:, at : at + 1]
            sums.append(o * (1.0 / total))
            left = top + jnp.log2(total)
            for step in range(3):
                piece = left.astype(bf16).astype(f32)
                left = left - piece
                extra = jnp.where(lane == 2 * step + head, piece, extra)
        out_ref[group, :tok, :] = jnp.where(lane < HS, sums[0], sums[1]).astype(bf16)
        lse_s[pl.ds(group * padded, tok), :] = extra
    turned = jnp.transpose(lse_s[...])[:8, :]
    for group in range(groups):
        for half in range(2):
            begin = group * padded + half * LANES
            out_ref[group, pl.ds(tok + 8 * half, 8), :] = turned[:, begin : begin + LANES].astype(bf16)


def attention_cost(queries, keys):
    return pl.CostEstimate(
        flops=2 * 2 * 2 * queries * keys * LANES, bytes_accessed=4 * queries * LANES, transcendentals=2 * queries * keys
    )


def attend_first(kv, q_all):
    blocks, tok2, _ = kv.shape
    groups, tok, _ = q_all.shape
    span, rows = blocks * tok2 // 2, groups * tok
    vmem = pl.BlockSpec(memory_space=pltpu.VMEM)
    return pl.pallas_call(
        first_kernel,
        out_shape=jax.ShapeDtypeStruct((2, rows, LANES), f32),
        in_specs=[vmem, vmem],
        out_specs=vmem,
        scratch_shapes=[pltpu.VMEM((span, LANES), bf16), pltpu.VMEM((2, span, LANES), bf16)],
        compiler_params=pltpu.CompilerParams(vmem_limit_bytes=16 * MIB),
        cost_estimate=attention_cost(rows, span),
        name="attend_own_core",
    )(kv, q_all)


def attend_second(kv, q_all, sums):
    blocks, tok2, _ = kv.shape
    groups, tok, _ = q_all.shape
    span, rows = blocks * tok2 // 2, groups * tok
    vmem = pl.BlockSpec(memory_space=pltpu.VMEM)
    return pl.pallas_call(
        second_kernel,
        out_shape=jax.ShapeDtypeStruct((groups, tok + EXTRA, LANES), bf16),
        in_specs=[vmem] * 3,
        out_specs=vmem,
        scratch_shapes=[
            pltpu.VMEM((span, LANES), bf16),
            pltpu.VMEM((2, span, LANES), bf16),
            pltpu.VMEM((groups * 2 * LANES, LANES), f32),
        ],
        compiler_params=pltpu.CompilerParams(vmem_limit_bytes=16 * MIB),
        cost_estimate=attention_cost(rows, span),
        name="attend_other_core",
    )(kv, q_all, sums)


def join_kernel(tiles, x_ref, _, tile_ref, cell_ref, splat_ref, out_ref, rows_s):
    groups, tok = x_ref.shape[0], x_ref.shape[1] - EXTRA
    width = 2 * LANES
    rows_s[...] = jnp.zeros_like(rows_s)
    rows_s[0:1, :tok] = splat_ref[...]
    halves = [x_ref[:, pl.ds(tok + 8 * half, 8), :].astype(f32) for half in range(2)]
    parts = jnp.concatenate(halves, axis=2)
    lse = parts + pltpu.roll(parts, 6, 1) + pltpu.roll(parts, 4, 1)
    top = jnp.max(lse, axis=0, keepdims=True)
    power = jnp.exp2(lse - top)
    weight = power * (rows_s[0:1, :] / jnp.sum(power, axis=0, keepdims=True))
    rows_s[: 8 * groups, :] = weight.reshape(8 * groups, width)
    tile = tile_ref[...].astype(f32)
    rows_s[64:65, :tok] = tile
    rows_s[65:66, :tok] = (cell_ref[...] + 1).astype(f32)
    columns = jnp.transpose(rows_s[...])[:tok, :]
    lane = lax.broadcasted_iota(jnp.int32, (tok, LANES), 1)
    weighted = jnp.zeros((tok, LANES), f32)
    for group in range(groups):
        by = jnp.where(lane < HS, columns[:, 8 * group : 8 * group + 1], columns[:, 8 * group + 1 : 8 * group + 2])
        weighted = weighted + x_ref[group, :tok, :].astype(f32) * by
    tile_column, cell_column = columns[:, 64:65], columns[:, 65:66]
    down = lax.broadcasted_iota(jnp.int32, (tok, tok), 0)
    across = lax.broadcasted_iota(jnp.int32, (tok, tok), 1)
    alike = jnp.where(tile_column == tile, 1.0, 0.0)
    rank_row = jnp.sum(jnp.where(down < across, alike, 0.0), axis=0, keepdims=True)
    rank_column = jnp.sum(jnp.where(across < down, alike, 0.0), axis=1, keepdims=True)
    cells = jnp.where(lane.astype(f32) == rank_column, cell_column, 0.0).astype(bf16)
    row = lax.broadcasted_iota(jnp.int32, (tiles * PIECE, tok), 0).astype(f32)
    main = jnp.where(row == tile * PIECE + rank_row, 1.0, 0.0).astype(bf16)
    tail = jnp.where(row == tile * PIECE + float(SLOTS), 1.0, 0.0).astype(bf16)
    out_ref[...] = (dot(main, weighted.astype(bf16)) + dot(tail, cells)).astype(bf16)


def join(received, early, tile, cell, splat_weight, tiles):
    vmem = pl.BlockSpec(memory_space=pltpu.VMEM)
    return pl.pallas_call(
        functools.partial(join_kernel, tiles),
        out_shape=jax.ShapeDtypeStruct((tiles * PIECE, LANES), bf16),
        in_specs=[vmem, pl.BlockSpec(memory_space=pl.ANY)] + [vmem] * 3,
        out_specs=vmem,
        scratch_shapes=[pltpu.VMEM((LANES, 2 * LANES), f32)],
        compiler_params=pltpu.CompilerParams(vmem_limit_bytes=8 * MIB),
        name="join_pack",
    )(received, early, tile, cell, splat_weight)


def splat_kernel(x_ref, out_ref, x_s, y_s, r_s):
    sources = x_ref.shape[0] // PIECE
    cells = out_ref.shape[1]
    x_s[...] = x_ref[...].astype(f32)
    y_s[...] = jnp.zeros_like(y_s)
    y_s[:sources, :] = x_s[pl.ds(SLOTS, sources, stride=PIECE), :]
    y_t = jnp.transpose(y_s[...])
    r_s[...] = jnp.zeros_like(r_s)
    for slot in range(SLOTS):
        r_s[pl.ds(slot * LANES, sources), :] = x_s[pl.ds(slot, sources, stride=PIECE), :].astype(bf16)
    cell = (lax.broadcasted_iota(jnp.int32, (cells, LANES), 0) + 1).astype(f32)
    hits = [jnp.where(cell == y_t[slot : slot + 1, :], 1.0, 0.0).astype(bf16) for slot in range(SLOTS)]
    features = dot(jnp.concatenate(hits, axis=1), r_s[...]).astype(bf16)
    for copy in range(out_ref.shape[0]):
        out_ref[copy] = features


def splat(received, cells, copies):
    rows = received.shape[0]
    vmem = pl.BlockSpec(memory_space=pltpu.VMEM)
    return pl.pallas_call(
        splat_kernel,
        out_shape=jax.ShapeDtypeStruct((copies, cells, LANES), bf16),
        in_specs=[vmem],
        out_specs=vmem,
        scratch_shapes=[
            pltpu.VMEM((rows, LANES), f32),
            pltpu.VMEM((LANES, LANES), f32),
            pltpu.VMEM((SLOTS * LANES, LANES), bf16),
        ],
        compiler_params=pltpu.CompilerParams(vmem_limit_bytes=8 * MIB),
        name="splat",
    )(received)


def mlp_kernel(own_ref, f_ref, near_ref, far_ref, base_ref, gain_ref, up_hbm, down_hbm, bev_ref, mix_ref, bev_s, up_ref, down_ref, sems):
    copies = [
        pltpu.make_async_copy(up_hbm, up_ref, sems.at[0]),
        pltpu.make_async_copy(down_hbm, down_ref, sems.at[1]),
    ]
    for copy in copies:
        copy.start()
    share = bev_ref.shape[0]
    own = own_ref[0]
    near = jnp.concatenate([f_ref[own], f_ref[own ^ 1]], axis=1)
    far = jnp.concatenate([f_ref[own ^ 2], f_ref[own ^ 3]], axis=1)
    depth = near.shape[1]
    bev = (
        base_ref[...].astype(f32)
        + dot(near, near_ref[...].reshape(depth, -1))
        + dot(far, far_ref[...].reshape(depth, -1))
    )
    bev_s[...] = bev
    mean_square = jnp.mean(bev * bev, axis=1, keepdims=True)
    normed = (bev * lax.rsqrt(mean_square + 1e-06) * gain_ref[...]).astype(bf16)
    bev_ref[...] = bev_s[pl.ds(pl.multiple_of(own * share, share), share), :]
    step = 256
    mixed = None
    copies[0].wait()
    for begin in range(0, up_ref.shape[1], step):
        u = dot(normed, up_ref[:, begin : begin + step])
        hidden = (0.5 * u * (1.0 + lax.erf(u * math.sqrt(0.5)))).astype(bf16)
        if begin == 0:
            copies[1].wait()
        term = dot(hidden, down_ref[begin : begin + step, :])
        mixed = term if mixed is None else mixed + term
    mix_ref[...] = mixed.astype(bf16)


def mlp(own, features, near, far, base, gain, up, down):
    heads = features.shape[0]
    cells, width = base.shape
    vmem, hbm = pl.BlockSpec(memory_space=pltpu.VMEM), pl.BlockSpec(memory_space=pl.ANY)
    return pl.pallas_call(
        mlp_kernel,
        out_shape=(
            jax.ShapeDtypeStruct((cells // heads, width), f32),
            jax.ShapeDtypeStruct((cells, width), bf16),
        ),
        in_specs=[pl.BlockSpec(memory_space=pltpu.SMEM)] + [vmem] * 5 + [hbm] * 2,
        out_specs=(vmem, vmem),
        scratch_shapes=[
            pltpu.VMEM((cells, width), f32),
            pltpu.VMEM(up.shape, bf16),
            pltpu.VMEM(down.shape, bf16),
            pltpu.SemaphoreType.DMA((2,)),
        ],
        compiler_params=pltpu.CompilerParams(vmem_limit_bytes=24 * MIB),
        name="project_mlp",
    )(own, features, near, far, base, gain, up, down)


def swap(x, axis, bit):
    return lax.ppermute(x, axis, [(i, i ^ bit) for i in range(lax.axis_size(axis))])


def body(
    queries,
    key_states,
    value_states,
    splat_weight,
    tile_of,
    cell_of,
    bev_base,
    norm_gain,
    out_weight,
    up_weight,
    down_weight,
):
    tok = queries.shape[1]
    tiles = lax.axis_size("z") * lax.axis_size("y") * lax.axis_size("core")
    groups = lax.axis_size("y")
    heads = lax.axis_size("head")
    cells = bev_base.shape[1]
    q_copies, kv = prologue(queries, key_states, value_states, groups)
    q_all = lax.all_to_all(q_copies, "y", 0, 0)
    near_weight = jnp.stack([out_weight, swap(out_weight, "head", 1)])
    own_kv = lax.all_gather(kv, "z")
    own_kv, q_all, near_weight = lax.optimization_barrier((own_kv, q_all, near_weight))
    other_kv = swap(own_kv, "core", 1)
    far_weight = swap(near_weight, "head", 2)
    sums = attend_first(own_kv, q_all)
    partial = attend_second(other_kv, q_all, sums)
    partial = lax.all_to_all(partial, "y", 0, 0)
    packed = join(partial, far_weight, tile_of.reshape(1, tok), cell_of, splat_weight, tiles)
    received = lax.all_to_all(packed.reshape(tiles, PIECE, LANES), ("z", "y", "core"), 0, 0)
    features = splat(received.reshape(tiles * PIECE, LANES), cells, heads)
    features = lax.all_to_all(features, "head", 0, 0)
    own = lax.axis_index("head").astype(jnp.int32).reshape(1)
    bev_rows, mixed = mlp(
        own, features, near_weight, far_weight, bev_base[0], norm_gain[None, :], up_weight, down_weight
    )
    mixed = lax.all_to_all(mixed.reshape(heads, cells // heads, mixed.shape[1]), "head", 0, 0)
    return (bev_rows + jnp.sum(mixed.astype(f32), axis=0)).astype(bf16)[None]


def solution(mesh):
    core, y = 2, 4
    z = mesh.shape["ctx"] // (core * y)
    split = Mesh(
        mesh.devices.reshape(z, y, core, mesh.shape["head"], mesh.shape["scene"]),
        ("z", "y", "core", "head", "scene"),
    )
    ctx = ("z", "y", "core")
    placed = (
        P("scene", ctx, "head"),
        P("scene", ctx, "head"),
        P("scene", ctx, "head"),
        P("scene", ctx),
        P("scene", ctx, None),
        P("scene", ctx),
        P("scene", ctx, None),
        P(),
        P("head", None),
        P(None, "head"),
        P("head", None),
    )
    return jax.shard_map(
        body,
        mesh=split,
        in_specs=placed,
        out_specs=P("scene", ctx + ("head",), None),
        check_vma=False,
    )
```

```python
import functools
import math

import jax
import jax.numpy as jnp
from jax import lax
from jax.experimental import pallas as pl
from jax.experimental.pallas import tpu as pltpu
from jax.sharding import Mesh
from jax.sharding import PartitionSpec as P

HS = 64
LANES = 128
SLOTS = 4
PIECE = 8
EXTRA = 16
EXPONENT = math.log2(math.e) / math.sqrt(HS)
MIB = 1024 * 1024

f32 = jnp.float32
bf16 = jnp.bfloat16


def dot(a, b):
    return lax.dot_general(a, b, (((1,), (0,)), ((), ())), preferred_element_type=f32)


def dot_nt(a, b):
    return lax.dot_general(a, b, (((1,), (1,)), ((), ())), preferred_element_type=f32)


def prologue_kernel(q_ref, k_ref, v_ref, q_out, kv_out):
    tok = q_ref.shape[1]
    for copy in range(q_out.shape[0]):
        q_out[copy] = q_ref[0]
    kv_out[:tok, :] = k_ref[0]
    kv_out[tok:, :] = v_ref[0]


def prologue(queries, key_states, value_states, copies):
    tok = queries.shape[1]
    vmem = pl.BlockSpec(memory_space=pltpu.VMEM)
    return pl.pallas_call(
        prologue_kernel,
        out_shape=(
            jax.ShapeDtypeStruct((copies, tok, LANES), bf16),
            jax.ShapeDtypeStruct((2 * tok, LANES), bf16),
        ),
        in_specs=[vmem] * 3,
        out_specs=(vmem, vmem),
        compiler_params=pltpu.CompilerParams(vmem_limit_bytes=58 * MIB),
        name="prologue",
    )(queries, key_states, value_states)


def attend_block(q_ref, group, k_s, v_s):
    low = lax.broadcasted_iota(jnp.int32, (1, LANES), 1) < HS
    q = q_ref[group]
    tok, span, step = q.shape[0], k_s.shape[0], 640
    keeps = [jnp.where(low if head == 0 else ~low, 1.0, 0.0).astype(bf16) for head in range(2)]
    s = dot_nt(jnp.concatenate([q * keep for keep in keeps], axis=0), k_s[...])
    top = jnp.max(s, axis=1, keepdims=True)
    sums = [None, None]
    for begin in range(0, span, step):
        p = jnp.exp2((s[:, begin : begin + step] - top) * EXPONENT).astype(bf16)
        for head in range(2):
            term = dot(p[head * tok : (head + 1) * tok], v_s[head, begin : begin + step, :])
            sums[head] = term if sums[head] is None else sums[head] + term
    return [(head, top[head * tok : (head + 1) * tok] * EXPONENT, sums[head]) for head in range(2)]


def stage_keys(kv_ref, k_s, v_s):
    blocks, tok = kv_ref.shape[0], kv_ref.shape[1] // 2
    span = blocks * tok
    low = jnp.where(lax.broadcasted_iota(jnp.int32, (1, LANES), 1) < HS, 1.0, 0.0)
    low_b, high_b = low.astype(bf16), (1.0 - low).astype(bf16)
    k_s[...] = kv_ref[:, :tok, :].reshape(span, LANES)
    values = kv_ref[:, tok:, :].reshape(span, LANES)
    v_s[0] = values * low_b + high_b
    v_s[1] = values * high_b + low_b


def other_half(head):
    return (LANES - 1, LANES - 2) if head == 0 else (0, 1)


def first_kernel(kv_ref, q_ref, sum_ref, k_s, v_s):
    groups, tok = q_ref.shape[0], q_ref.shape[1]
    stage_keys(kv_ref, k_s, v_s)
    lane = lax.broadcasted_iota(jnp.int32, (1, LANES), 1)
    for group in range(groups):
        for head, top, sums in attend_block(q_ref, group, k_s, v_s):
            sum_ref[head, pl.ds(group * tok, tok), :] = jnp.where(lane == other_half(head)[1], top, sums)


def second_kernel(kv_ref, q_ref, sum_ref, out_ref, k_s, v_s, lse_s):
    groups, tok = q_ref.shape[0], q_ref.shape[1]
    padded = lse_s.shape[0] // groups
    stage_keys(kv_ref, k_s, v_s)
    lane = lax.broadcasted_iota(jnp.int32, (tok, LANES), 1)
    lse_s[...] = jnp.zeros_like(lse_s)
    for group in range(groups):
        sums = []
        extra = jnp.zeros((tok, LANES), f32)
        for head, top_b, sum_b in attend_block(q_ref, group, k_s, v_s):
            at, top_at = other_half(head)
            sum_a = sum_ref[head, pl.ds(group * tok, tok), :]
            top_a = sum_a[:, top_at : top_at + 1]
            top = jnp.maximum(top_a, top_b)
            o = sum_a * jnp.exp2(top_a - top) + sum_b * jnp.exp2(top_b - top)
            total = o[:, at : at + 1]
            sums.append(o * (1.0 / total))
            left = top + jnp.log2(total)
            for step in range(3):
                piece = left.astype(bf16).astype(f32)
                left = left - piece
                extra = jnp.where(lane == 2 * step + head, piece, extra)
        out_ref[group, :tok, :] = jnp.where(lane < HS, sums[0], sums[1]).astype(bf16)
        lse_s[pl.ds(group * padded, tok), :] = extra
    turned = jnp.transpose(lse_s[...])[:8, :]
    for group in range(groups):
        for half in range(2):
            begin = group * padded + half * LANES
            out_ref[group, pl.ds(tok + 8 * half, 8), :] = turned[:, begin : begin + LANES].astype(bf16)


def attention_cost(queries, keys):
    return pl.CostEstimate(
        flops=2 * 2 * 2 * queries * keys * LANES, bytes_accessed=4 * queries * LANES, transcendentals=2 * queries * keys
    )


def attend_first(kv, q_all):
    blocks, tok2, _ = kv.shape
    groups, tok, _ = q_all.shape
    span, rows = blocks * tok2 // 2, groups * tok
    vmem = pl.BlockSpec(memory_space=pltpu.VMEM)
    return pl.pallas_call(
        first_kernel,
        out_shape=jax.ShapeDtypeStruct((2, rows, LANES), f32),
        in_specs=[vmem, vmem],
        out_specs=vmem,
        scratch_shapes=[pltpu.VMEM((span, LANES), bf16), pltpu.VMEM((2, span, LANES), bf16)],
        compiler_params=pltpu.CompilerParams(vmem_limit_bytes=16 * MIB),
        cost_estimate=attention_cost(rows, span),
        name="attend_own_core",
    )(kv, q_all)


def attend_second(kv, q_all, sums):
    blocks, tok2, _ = kv.shape
    groups, tok, _ = q_all.shape
    span, rows = blocks * tok2 // 2, groups * tok
    vmem = pl.BlockSpec(memory_space=pltpu.VMEM)
    return pl.pallas_call(
        second_kernel,
        out_shape=jax.ShapeDtypeStruct((groups, tok + EXTRA, LANES), bf16),
        in_specs=[vmem] * 3,
        out_specs=vmem,
        scratch_shapes=[
            pltpu.VMEM((span, LANES), bf16),
            pltpu.VMEM((2, span, LANES), bf16),
            pltpu.VMEM((groups * 2 * LANES, LANES), f32),
        ],
        compiler_params=pltpu.CompilerParams(vmem_limit_bytes=16 * MIB),
        cost_estimate=attention_cost(rows, span),
        name="attend_other_core",
    )(kv, q_all, sums)


def join_kernel(tiles, x_ref, _, tile_ref, cell_ref, splat_ref, out_ref, rows_s):
    groups, tok = x_ref.shape[0], x_ref.shape[1] - EXTRA
    width = 2 * LANES
    rows_s[...] = jnp.zeros_like(rows_s)
    rows_s[0:1, :tok] = splat_ref[...]
    halves = [x_ref[:, pl.ds(tok + 8 * half, 8), :].astype(f32) for half in range(2)]
    parts = jnp.concatenate(halves, axis=2)
    lse = parts + pltpu.roll(parts, 6, 1) + pltpu.roll(parts, 4, 1)
    top = jnp.max(lse, axis=0, keepdims=True)
    power = jnp.exp2(lse - top)
    weight = power * (rows_s[0:1, :] / jnp.sum(power, axis=0, keepdims=True))
    rows_s[: 8 * groups, :] = weight.reshape(8 * groups, width)
    tile = tile_ref[...].astype(f32)
    rows_s[64:65, :tok] = tile
    rows_s[65:66, :tok] = (cell_ref[...] + 1).astype(f32)
    columns = jnp.transpose(rows_s[...])[:tok, :]
    lane = lax.broadcasted_iota(jnp.int32, (tok, LANES), 1)
    weighted = jnp.zeros((tok, LANES), f32)
    for group in range(groups):
        by = jnp.where(lane < HS, columns[:, 8 * group : 8 * group + 1], columns[:, 8 * group + 1 : 8 * group + 2])
        weighted = weighted + x_ref[group, :tok, :].astype(f32) * by
    tile_column, cell_column = columns[:, 64:65], columns[:, 65:66]
    down = lax.broadcasted_iota(jnp.int32, (tok, tok), 0)
    across = lax.broadcasted_iota(jnp.int32, (tok, tok), 1)
    alike = jnp.where(tile_column == tile, 1.0, 0.0)
    rank_row = jnp.sum(jnp.where(down < across, alike, 0.0), axis=0, keepdims=True)
    rank_column = jnp.sum(jnp.where(across < down, alike, 0.0), axis=1, keepdims=True)
    cells = jnp.where(lane.astype(f32) == rank_column, cell_column, 0.0).astype(bf16)
    row = lax.broadcasted_iota(jnp.int32, (tiles * PIECE, tok), 0).astype(f32)
    main = jnp.where(row == tile * PIECE + rank_row, 1.0, 0.0).astype(bf16)
    tail = jnp.where(row == tile * PIECE + float(SLOTS), 1.0, 0.0).astype(bf16)
    out_ref[...] = (dot(main, weighted.astype(bf16)) + dot(tail, cells)).astype(bf16)


def join(received, early, tile, cell, splat_weight, tiles):
    vmem = pl.BlockSpec(memory_space=pltpu.VMEM)
    return pl.pallas_call(
        functools.partial(join_kernel, tiles),
        out_shape=jax.ShapeDtypeStruct((tiles * PIECE, LANES), bf16),
        in_specs=[vmem, pl.BlockSpec(memory_space=pl.ANY)] + [vmem] * 3,
        out_specs=vmem,
        scratch_shapes=[pltpu.VMEM((LANES, 2 * LANES), f32)],
        compiler_params=pltpu.CompilerParams(vmem_limit_bytes=8 * MIB),
        name="join_pack",
    )(received, early, tile, cell, splat_weight)


def splat_kernel(x_ref, out_ref, x_s, y_s, r_s):
    sources = x_ref.shape[0] // PIECE
    cells = out_ref.shape[1]
    x_s[...] = x_ref[...].astype(f32)
    y_s[...] = jnp.zeros_like(y_s)
    y_s[:sources, :] = x_s[pl.ds(SLOTS, sources, stride=PIECE), :]
    y_t = jnp.transpose(y_s[...])
    r_s[...] = jnp.zeros_like(r_s)
    for slot in range(SLOTS):
        r_s[pl.ds(slot * LANES, sources), :] = x_s[pl.ds(slot, sources, stride=PIECE), :].astype(bf16)
    cell = (lax.broadcasted_iota(jnp.int32, (cells, LANES), 0) + 1).astype(f32)
    hits = [jnp.where(cell == y_t[slot : slot + 1, :], 1.0, 0.0).astype(bf16) for slot in range(SLOTS)]
    features = dot(jnp.concatenate(hits, axis=1), r_s[...]).astype(bf16)
    for copy in range(out_ref.shape[0]):
        out_ref[copy] = features


def splat(received, cells, copies):
    rows = received.shape[0]
    vmem = pl.BlockSpec(memory_space=pltpu.VMEM)
    return pl.pallas_call(
        splat_kernel,
        out_shape=jax.ShapeDtypeStruct((copies, cells, LANES), bf16),
        in_specs=[vmem],
        out_specs=vmem,
        scratch_shapes=[
            pltpu.VMEM((rows, LANES), f32),
            pltpu.VMEM((LANES, LANES), f32),
            pltpu.VMEM((SLOTS * LANES, LANES), bf16),
        ],
        compiler_params=pltpu.CompilerParams(vmem_limit_bytes=8 * MIB),
        name="splat",
    )(received)


def mlp_kernel(own_ref, f_ref, near_ref, far_ref, base_hbm, gain_ref, up_ref, down_hbm, bev_ref, mix_ref, bev_s, base_s, down_s, sems):
    base_copy = pltpu.make_async_copy(base_hbm, base_s, sems.at[0])
    down_copy = pltpu.make_async_copy(down_hbm, down_s, sems.at[1])
    base_copy.start()
    down_copy.start()
    share = bev_ref.shape[0]
    own = own_ref[0]
    near = jnp.concatenate([f_ref[own], f_ref[own ^ 1]], axis=1)
    far = jnp.concatenate([f_ref[own ^ 2], f_ref[own ^ 3]], axis=1)
    depth = near.shape[1]
    projected = dot(near, near_ref[...].reshape(depth, -1)) + dot(far, far_ref[...].reshape(depth, -1))
    base_copy.wait()
    bev = base_s[...].astype(f32) + projected
    bev_s[...] = bev
    mean_square = jnp.mean(bev * bev, axis=1, keepdims=True)
    normed = (bev * lax.rsqrt(mean_square + 1e-06) * gain_ref[...]).astype(bf16)
    bev_ref[...] = bev_s[pl.ds(pl.multiple_of(own * share, share), share), :]
    step = 256
    mixed = None
    for begin in range(0, up_ref.shape[1], step):
        u = dot(normed, up_ref[:, begin : begin + step])
        hidden = (0.5 * u * (1.0 + lax.erf(u * math.sqrt(0.5)))).astype(bf16)
        if begin == 0:
            down_copy.wait()
        term = dot(hidden, down_s[begin : begin + step, :])
        mixed = term if mixed is None else mixed + term
    mix_ref[...] = mixed.astype(bf16)


def mlp(own, features, near, far, base, gain, up, down):
    heads = features.shape[0]
    cells, width = base.shape
    vmem, hbm = pl.BlockSpec(memory_space=pltpu.VMEM), pl.BlockSpec(memory_space=pltpu.HBM)
    return pl.pallas_call(
        mlp_kernel,
        out_shape=(
            jax.ShapeDtypeStruct((cells // heads, width), f32),
            jax.ShapeDtypeStruct((cells, width), bf16),
        ),
        in_specs=[pl.BlockSpec(memory_space=pltpu.SMEM)] + [vmem] * 3 + [hbm, vmem, vmem, hbm],
        out_specs=(vmem, vmem),
        scratch_shapes=[
            pltpu.VMEM((cells, width), f32),
            pltpu.VMEM((cells, width), bf16),
            pltpu.VMEM(down.shape, bf16),
            pltpu.SemaphoreType.DMA((2,)),
        ],
        compiler_params=pltpu.CompilerParams(vmem_limit_bytes=20 * MIB),
        name="project_mlp",
    )(
        own,
        features,
        near,
        far,
        pltpu.with_memory_space_constraint(base, pltpu.HBM),
        gain,
        up,
        pltpu.with_memory_space_constraint(down, pltpu.HBM),
    )


def swap(x, axis, bit):
    return lax.ppermute(x, axis, [(i, i ^ bit) for i in range(lax.axis_size(axis))])


def body(
    queries,
    key_states,
    value_states,
    splat_weight,
    tile_of,
    cell_of,
    bev_base,
    norm_gain,
    out_weight,
    up_weight,
    down_weight,
):
    tok = queries.shape[1]
    tiles = lax.axis_size("z") * lax.axis_size("y") * lax.axis_size("core")
    groups = lax.axis_size("y")
    heads = lax.axis_size("head")
    cells = bev_base.shape[1]
    q_copies, kv = prologue(queries, key_states, value_states, groups)
    q_all = lax.all_to_all(q_copies, "y", 0, 0)
    near_weight = jnp.stack([out_weight, swap(out_weight, "head", 1)])
    own_kv = lax.all_gather(kv, "z")
    own_kv, q_all, near_weight = lax.optimization_barrier((own_kv, q_all, near_weight))
    other_kv = swap(own_kv, "core", 1)
    far_weight = swap(near_weight, "head", 2)
    sums = attend_first(own_kv, q_all)
    partial = attend_second(other_kv, q_all, sums)
    partial = lax.all_to_all(partial, "y", 0, 0)
    packed = join(partial, far_weight, tile_of.reshape(1, tok), cell_of, splat_weight, tiles)
    received = lax.all_to_all(packed.reshape(tiles, PIECE, LANES), ("z", "y", "core"), 0, 0)
    features = splat(received.reshape(tiles * PIECE, LANES), cells, heads)
    features = lax.all_to_all(features, "head", 0, 0)
    own = lax.axis_index("head").astype(jnp.int32).reshape(1)
    bev_rows, mixed = mlp(
        own, features, near_weight, far_weight, bev_base[0], norm_gain[None, :], up_weight, down_weight
    )
    mixed = lax.all_to_all(mixed.reshape(heads, cells // heads, mixed.shape[1]), "head", 0, 0)
    return (bev_rows + jnp.sum(mixed.astype(f32), axis=0)).astype(bf16)[None]


def solution(mesh):
    core, y = 2, 4
    z = mesh.shape["ctx"] // (core * y)
    split = Mesh(
        mesh.devices.reshape(z, y, core, mesh.shape["head"], mesh.shape["scene"]),
        ("z", "y", "core", "head", "scene"),
    )
    ctx = ("z", "y", "core")
    placed = (
        P("scene", ctx, "head"),
        P("scene", ctx, "head"),
        P("scene", ctx, "head"),
        P("scene", ctx),
        P("scene", ctx, None),
        P("scene", ctx),
        P("scene", ctx, None),
        P(),
        P("head", None),
        P(None, "head"),
        P("head", None),
    )
    return jax.shard_map(
        body,
        mesh=split,
        in_specs=placed,
        out_specs=P("scene", ctx + ("head",), None),
        check_vma=False,
    )
```

```python
import functools
import math

import jax
import jax.numpy as jnp
from jax import lax
from jax.experimental import pallas as pl
from jax.experimental.pallas import tpu as pltpu
from jax.sharding import Mesh
from jax.sharding import PartitionSpec as P

HS = 64
LANES = 128
SLOTS = 4
PIECE = 8
EXTRA = 16
EXPONENT = math.log2(math.e) / math.sqrt(HS)
MIB = 1024 * 1024

f32 = jnp.float32
bf16 = jnp.bfloat16


def dot(a, b):
    return lax.dot_general(a, b, (((1,), (0,)), ((), ())), preferred_element_type=f32)


def dot_nt(a, b):
    return lax.dot_general(a, b, (((1,), (1,)), ((), ())), preferred_element_type=f32)


def prologue_kernel(q_ref, k_ref, v_ref, q_out, kv_out):
    tok = q_ref.shape[1]
    for copy in range(q_out.shape[0]):
        q_out[copy] = q_ref[0]
    kv_out[:tok, :] = k_ref[0]
    kv_out[tok:, :] = v_ref[0]


def prologue(queries, key_states, value_states, copies):
    tok = queries.shape[1]
    vmem = pl.BlockSpec(memory_space=pltpu.VMEM)
    return pl.pallas_call(
        prologue_kernel,
        out_shape=(
            jax.ShapeDtypeStruct((copies, tok, LANES), bf16),
            jax.ShapeDtypeStruct((2 * tok, LANES), bf16),
        ),
        in_specs=[vmem] * 3,
        out_specs=(vmem, vmem),
        compiler_params=pltpu.CompilerParams(vmem_limit_bytes=58 * MIB),
        name="prologue",
    )(queries, key_states, value_states)


def attend_block(q_ref, group, k_s, v_s):
    low = lax.broadcasted_iota(jnp.int32, (1, LANES), 1) < HS
    q = q_ref[group]
    tok, span, step = q.shape[0], k_s.shape[0], 640
    keeps = [jnp.where(low if head == 0 else ~low, 1.0, 0.0).astype(bf16) for head in range(2)]
    s = dot_nt(jnp.concatenate([q * keep for keep in keeps], axis=0), k_s[...])
    top = jnp.max(s, axis=1, keepdims=True)
    sums = [None, None]
    for begin in range(0, span, step):
        p = jnp.exp2((s[:, begin : begin + step] - top) * EXPONENT).astype(bf16)
        for head in range(2):
            term = dot(p[head * tok : (head + 1) * tok], v_s[head, begin : begin + step, :])
            sums[head] = term if sums[head] is None else sums[head] + term
    return [(head, top[head * tok : (head + 1) * tok] * EXPONENT, sums[head]) for head in range(2)]


def stage_keys(kv_ref, k_s, v_s):
    blocks, tok = kv_ref.shape[0], kv_ref.shape[1] // 2
    span = blocks * tok
    low = jnp.where(lax.broadcasted_iota(jnp.int32, (1, LANES), 1) < HS, 1.0, 0.0)
    low_b, high_b = low.astype(bf16), (1.0 - low).astype(bf16)
    k_s[...] = kv_ref[:, :tok, :].reshape(span, LANES)
    values = kv_ref[:, tok:, :].reshape(span, LANES)
    v_s[0] = values * low_b + high_b
    v_s[1] = values * high_b + low_b


def other_half(head):
    return (LANES - 1, LANES - 2) if head == 0 else (0, 1)


def first_kernel(kv_ref, q_ref, sum_ref, k_s, v_s):
    groups, tok = q_ref.shape[0], q_ref.shape[1]
    stage_keys(kv_ref, k_s, v_s)
    lane = lax.broadcasted_iota(jnp.int32, (1, LANES), 1)
    for group in range(groups):
        for head, top, sums in attend_block(q_ref, group, k_s, v_s):
            sum_ref[head, pl.ds(group * tok, tok), :] = jnp.where(lane == other_half(head)[1], top, sums)


def second_kernel(kv_ref, q_ref, sum_ref, out_ref, k_s, v_s, lse_s):
    groups, tok = q_ref.shape[0], q_ref.shape[1]
    padded = lse_s.shape[0] // groups
    stage_keys(kv_ref, k_s, v_s)
    lane = lax.broadcasted_iota(jnp.int32, (tok, LANES), 1)
    lse_s[...] = jnp.zeros_like(lse_s)
    for group in range(groups):
        sums = []
        extra = jnp.zeros((tok, LANES), f32)
        for head, top_b, sum_b in attend_block(q_ref, group, k_s, v_s):
            at, top_at = other_half(head)
            sum_a = sum_ref[head, pl.ds(group * tok, tok), :]
            top_a = sum_a[:, top_at : top_at + 1]
            top = jnp.maximum(top_a, top_b)
            o = sum_a * jnp.exp2(top_a - top) + sum_b * jnp.exp2(top_b - top)
            total = o[:, at : at + 1]
            sums.append(o * (1.0 / total))
            left = top + jnp.log2(total)
            for step in range(3):
                piece = left.astype(bf16).astype(f32)
                left = left - piece
                extra = jnp.where(lane == 2 * step + head, piece, extra)
        out_ref[group, :tok, :] = jnp.where(lane < HS, sums[0], sums[1]).astype(bf16)
        lse_s[pl.ds(group * padded, tok), :] = extra
    turned = jnp.transpose(lse_s[...])[:8, :]
    for group in range(groups):
        for half in range(2):
            begin = group * padded + half * LANES
            out_ref[group, pl.ds(tok + 8 * half, 8), :] = turned[:, begin : begin + LANES].astype(bf16)


def attention_cost(queries, keys):
    return pl.CostEstimate(
        flops=2 * 2 * 2 * queries * keys * LANES, bytes_accessed=4 * queries * LANES, transcendentals=2 * queries * keys
    )


def attend_first(kv, q_all):
    blocks, tok2, _ = kv.shape
    groups, tok, _ = q_all.shape
    span, rows = blocks * tok2 // 2, groups * tok
    vmem = pl.BlockSpec(memory_space=pltpu.VMEM)
    return pl.pallas_call(
        first_kernel,
        out_shape=jax.ShapeDtypeStruct((2, rows, LANES), f32),
        in_specs=[vmem, vmem],
        out_specs=vmem,
        scratch_shapes=[pltpu.VMEM((span, LANES), bf16), pltpu.VMEM((2, span, LANES), bf16)],
        compiler_params=pltpu.CompilerParams(vmem_limit_bytes=16 * MIB),
        cost_estimate=attention_cost(rows, span),
        name="attend_own_core",
    )(kv, q_all)


def attend_second(kv, q_all, sums):
    blocks, tok2, _ = kv.shape
    groups, tok, _ = q_all.shape
    span, rows = blocks * tok2 // 2, groups * tok
    vmem = pl.BlockSpec(memory_space=pltpu.VMEM)
    return pl.pallas_call(
        second_kernel,
        out_shape=jax.ShapeDtypeStruct((groups, tok + EXTRA, LANES), bf16),
        in_specs=[vmem] * 3,
        out_specs=vmem,
        scratch_shapes=[
            pltpu.VMEM((span, LANES), bf16),
            pltpu.VMEM((2, span, LANES), bf16),
            pltpu.VMEM((groups * 2 * LANES, LANES), f32),
        ],
        compiler_params=pltpu.CompilerParams(vmem_limit_bytes=16 * MIB),
        cost_estimate=attention_cost(rows, span),
        name="attend_other_core",
    )(kv, q_all, sums)


def join_kernel(tiles, x_ref, tile_ref, cell_ref, splat_ref, out_ref, rows_s):
    groups, tok = x_ref.shape[0], x_ref.shape[1] - EXTRA
    width = 2 * LANES
    rows_s[...] = jnp.zeros_like(rows_s)
    rows_s[0:1, :tok] = splat_ref[...]
    halves = [x_ref[:, pl.ds(tok + 8 * half, 8), :].astype(f32) for half in range(2)]
    parts = jnp.concatenate(halves, axis=2)
    lse = parts + pltpu.roll(parts, 6, 1) + pltpu.roll(parts, 4, 1)
    top = jnp.max(lse, axis=0, keepdims=True)
    power = jnp.exp2(lse - top)
    weight = power * (rows_s[0:1, :] / jnp.sum(power, axis=0, keepdims=True))
    rows_s[: 8 * groups, :] = weight.reshape(8 * groups, width)
    tile = tile_ref[...].astype(f32)
    rows_s[64:65, :tok] = tile
    rows_s[65:66, :tok] = (cell_ref[...] + 1).astype(f32)
    columns = jnp.transpose(rows_s[...])[:tok, :]
    lane = lax.broadcasted_iota(jnp.int32, (tok, LANES), 1)
    weighted = jnp.zeros((tok, LANES), f32)
    for group in range(groups):
        by = jnp.where(lane < HS, columns[:, 8 * group : 8 * group + 1], columns[:, 8 * group + 1 : 8 * group + 2])
        weighted = weighted + x_ref[group, :tok, :].astype(f32) * by
    tile_column, cell_column = columns[:, 64:65], columns[:, 65:66]
    down = lax.broadcasted_iota(jnp.int32, (tok, tok), 0)
    across = lax.broadcasted_iota(jnp.int32, (tok, tok), 1)
    alike = jnp.where(tile_column == tile, 1.0, 0.0)
    rank_row = jnp.sum(jnp.where(down < across, alike, 0.0), axis=0, keepdims=True)
    rank_column = jnp.sum(jnp.where(across < down, alike, 0.0), axis=1, keepdims=True)
    cells = jnp.where(lane.astype(f32) == rank_column, cell_column, 0.0).astype(bf16)
    row = lax.broadcasted_iota(jnp.int32, (tiles * PIECE, tok), 0).astype(f32)
    main = jnp.where(row == tile * PIECE + rank_row, 1.0, 0.0).astype(bf16)
    tail = jnp.where(row == tile * PIECE + float(SLOTS), 1.0, 0.0).astype(bf16)
    out_ref[...] = (dot(main, weighted.astype(bf16)) + dot(tail, cells)).astype(bf16)


def join(received, tile, cell, splat_weight, tiles):
    vmem = pl.BlockSpec(memory_space=pltpu.VMEM)
    return pl.pallas_call(
        functools.partial(join_kernel, tiles),
        out_shape=jax.ShapeDtypeStruct((tiles * PIECE, LANES), bf16),
        in_specs=[vmem] * 4,
        out_specs=vmem,
        scratch_shapes=[pltpu.VMEM((LANES, 2 * LANES), f32)],
        compiler_params=pltpu.CompilerParams(vmem_limit_bytes=8 * MIB),
        name="join_pack",
    )(received, tile, cell, splat_weight)


def splat_kernel(x_ref, *refs):
    out_ref, x_s, y_s, r_s = refs[-4:]
    sources = x_ref.shape[0] // PIECE
    cells = out_ref.shape[1]
    x_s[...] = x_ref[...].astype(f32)
    y_s[...] = jnp.zeros_like(y_s)
    y_s[:sources, :] = x_s[pl.ds(SLOTS, sources, stride=PIECE), :]
    y_t = jnp.transpose(y_s[...])
    r_s[...] = jnp.zeros_like(r_s)
    for slot in range(SLOTS):
        r_s[pl.ds(slot * LANES, sources), :] = x_s[pl.ds(slot, sources, stride=PIECE), :].astype(bf16)
    cell = (lax.broadcasted_iota(jnp.int32, (cells, LANES), 0) + 1).astype(f32)
    hits = [jnp.where(cell == y_t[slot : slot + 1, :], 1.0, 0.0).astype(bf16) for slot in range(SLOTS)]
    features = dot(jnp.concatenate(hits, axis=1), r_s[...]).astype(bf16)
    for copy in range(out_ref.shape[0]):
        out_ref[copy] = features


def splat(received, early, cells, copies):
    rows = received.shape[0]
    vmem = pl.BlockSpec(memory_space=pltpu.VMEM)
    return pl.pallas_call(
        splat_kernel,
        out_shape=jax.ShapeDtypeStruct((copies, cells, LANES), bf16),
        in_specs=[vmem] + [pl.BlockSpec(memory_space=pl.ANY)] * len(early),
        out_specs=vmem,
        scratch_shapes=[
            pltpu.VMEM((rows, LANES), f32),
            pltpu.VMEM((LANES, LANES), f32),
            pltpu.VMEM((SLOTS * LANES, LANES), bf16),
        ],
        compiler_params=pltpu.CompilerParams(vmem_limit_bytes=8 * MIB),
        name="splat",
    )(received, *early)


def mlp_kernel(own_ref, *refs):
    weights, (f_ref, base_hbm, gain_ref, up_ref, down_hbm) = refs[:4], refs[4:9]
    bev_ref, mix_ref, bev_s, base_s, down_s, sems = refs[9:]
    base_copy = pltpu.make_async_copy(base_hbm, base_s, sems.at[0])
    down_copy = pltpu.make_async_copy(down_hbm, down_s, sems.at[1])
    base_copy.start()
    down_copy.start()
    share = bev_ref.shape[0]
    own = own_ref[0]
    projected = None
    for k in range(0, len(weights), 2):
        features = jnp.concatenate([f_ref[own ^ k], f_ref[own ^ (k + 1)]], axis=1)
        term = dot(features, jnp.concatenate([weights[k][...], weights[k + 1][...]], axis=0))
        projected = term if projected is None else projected + term
    base_copy.wait()
    bev = base_s[...].astype(f32) + projected
    bev_s[...] = bev
    mean_square = jnp.mean(bev * bev, axis=1, keepdims=True)
    normed = (bev * lax.rsqrt(mean_square + 1e-06) * gain_ref[...]).astype(bf16)
    bev_ref[...] = bev_s[pl.ds(pl.multiple_of(own * share, share), share), :]
    step = 256
    mixed = None
    for begin in range(0, up_ref.shape[1], step):
        u = dot(normed, up_ref[:, begin : begin + step])
        hidden = (0.5 * u * (1.0 + lax.erf(u * math.sqrt(0.5)))).astype(bf16)
        if begin == 0:
            down_copy.wait()
        term = dot(hidden, down_s[begin : begin + step, :])
        mixed = term if mixed is None else mixed + term
    mix_ref[...] = mixed.astype(bf16)


def mlp(own, weights, features, base, gain, up, down):
    heads = features.shape[0]
    cells, width = base.shape
    vmem, hbm = pl.BlockSpec(memory_space=pltpu.VMEM), pl.BlockSpec(memory_space=pltpu.HBM)
    return pl.pallas_call(
        mlp_kernel,
        out_shape=(
            jax.ShapeDtypeStruct((cells // heads, width), f32),
            jax.ShapeDtypeStruct((cells, width), bf16),
        ),
        in_specs=[pl.BlockSpec(memory_space=pltpu.SMEM)] + [vmem] * 5 + [hbm, vmem, vmem, hbm],
        out_specs=(vmem, vmem),
        scratch_shapes=[
            pltpu.VMEM((cells, width), f32),
            pltpu.VMEM((cells, width), bf16),
            pltpu.VMEM(down.shape, bf16),
            pltpu.SemaphoreType.DMA((2,)),
        ],
        compiler_params=pltpu.CompilerParams(vmem_limit_bytes=20 * MIB),
        name="project_mlp",
    )(
        own,
        *weights,
        features,
        pltpu.with_memory_space_constraint(base, pltpu.HBM),
        gain,
        up,
        pltpu.with_memory_space_constraint(down, pltpu.HBM),
    )


def swap(x, axis, bit):
    return lax.ppermute(x, axis, [(i, i ^ bit) for i in range(lax.axis_size(axis))])


def body(
    queries,
    key_states,
    value_states,
    splat_weight,
    tile_of,
    cell_of,
    bev_base,
    norm_gain,
    out_weight,
    up_weight,
    down_weight,
):
    tok = queries.shape[1]
    tiles = lax.axis_size("z") * lax.axis_size("y") * lax.axis_size("core")
    groups = lax.axis_size("y")
    heads = lax.axis_size("head")
    cells = bev_base.shape[1]
    q_copies, kv = prologue(queries, key_states, value_states, groups)
    q_all = lax.all_to_all(q_copies, "y", 0, 0)
    own_kv = lax.all_gather(kv, "z")
    own_kv, q_all = lax.optimization_barrier((own_kv, q_all))
    other_kv = swap(own_kv, "core", 1)
    sums = attend_first(own_kv, q_all)
    partial = attend_second(other_kv, q_all, sums)
    partial = lax.all_to_all(partial, "y", 0, 0)
    packed = join(partial, tile_of.reshape(1, tok), cell_of, splat_weight, tiles)
    packed, out_weight = lax.optimization_barrier((packed, out_weight))
    weights = tuple(swap(out_weight, "head", k) for k in range(heads - 1, 0, -1))[::-1]
    received = lax.all_to_all(packed.reshape(tiles, PIECE, LANES), ("z", "y", "core"), 0, 0)
    features = splat(received.reshape(tiles * PIECE, LANES), weights, cells, heads)
    features = lax.all_to_all(features, "head", 0, 0)
    own = lax.axis_index("head").astype(jnp.int32).reshape(1)
    bev_rows, mixed = mlp(
        own, (out_weight,) + weights, features, bev_base[0], norm_gain[None, :], up_weight, down_weight
    )
    mixed = lax.all_to_all(mixed.reshape(heads, cells // heads, mixed.shape[1]), "head", 0, 0)
    return (bev_rows + jnp.sum(mixed.astype(f32), axis=0)).astype(bf16)[None]


def solution(mesh):
    core, y = 2, 4
    z = mesh.shape["ctx"] // (core * y)
    split = Mesh(
        mesh.devices.reshape(z, y, core, mesh.shape["head"], mesh.shape["scene"]),
        ("z", "y", "core", "head", "scene"),
    )
    ctx = ("z", "y", "core")
    placed = (
        P("scene", ctx, "head"),
        P("scene", ctx, "head"),
        P("scene", ctx, "head"),
        P("scene", ctx),
        P("scene", ctx, None),
        P("scene", ctx),
        P("scene", ctx, None),
        P(),
        P("head", None),
        P(None, "head"),
        P("head", None),
    )
    return jax.shard_map(
        body,
        mesh=split,
        in_specs=placed,
        out_specs=P("scene", ctx + ("head",), None),
        check_vma=False,
    )
```

```python
import functools
import math

import jax
import jax.numpy as jnp
from jax import lax
from jax.experimental import pallas as pl
from jax.experimental.pallas import tpu as pltpu
from jax.sharding import Mesh
from jax.sharding import PartitionSpec as P

HS = 64
LANES = 128
SLOTS = 4
PIECE = 24
EXPONENT = math.log2(math.e) / math.sqrt(HS)
MIB = 1024 * 1024

f32 = jnp.float32
bf16 = jnp.bfloat16


def dot(a, b):
    return lax.dot_general(a, b, (((1,), (0,)), ((), ())), preferred_element_type=f32)


def dot_nt(a, b):
    return lax.dot_general(a, b, (((1,), (1,)), ((), ())), preferred_element_type=f32)


def prologue_kernel(q_ref, k_ref, v_ref, tile_ref, cell_ref, splat_ref, q_out, kv_out, rows_s):
    copies, tok = q_out.shape[0], q_out.shape[1]
    tile = tile_ref[...].astype(f32)
    coarse = splat_ref[...].astype(bf16).astype(f32)
    rows_s[...] = jnp.zeros_like(rows_s)
    rows_s[0:1, :tok] = tile
    rows_s[2:3, :tok] = (cell_ref[...] + 1).astype(f32)
    rows_s[3:4, :tok] = coarse
    rows_s[4:5, :tok] = splat_ref[...] - coarse
    columns = jnp.transpose(rows_s[...])[:tok, :]
    shape = (tok, tok)
    earlier = lax.broadcasted_iota(jnp.int32, shape, 1) < lax.broadcasted_iota(jnp.int32, shape, 0)
    alike = jnp.where(columns[:, 0:1] == tile, 1.0, 0.0)
    rank = jnp.sum(jnp.where(earlier, alike, 0.0), axis=1, keepdims=True)
    lane = lax.broadcasted_iota(jnp.int32, (tok, LANES), 1)
    meta = jnp.where(lane == 1, rank, columns).astype(bf16)
    for copy in range(copies):
        q_out[copy, :, :LANES] = q_ref[0]
        q_out[copy, :, LANES:] = meta
    kv_out[:tok, :] = k_ref[0]
    kv_out[tok:, :] = v_ref[0]


def prologue(queries, key_states, value_states, tile, cell, splat_weight, copies):
    tok = queries.shape[1]
    vmem = pl.BlockSpec(memory_space=pltpu.VMEM)
    return pl.pallas_call(
        prologue_kernel,
        out_shape=(
            jax.ShapeDtypeStruct((copies, tok, 2 * LANES), bf16),
            jax.ShapeDtypeStruct((2 * tok, LANES), bf16),
        ),
        in_specs=[vmem] * 6,
        out_specs=(vmem, vmem),
        scratch_shapes=[pltpu.VMEM((LANES, 2 * LANES), f32)],
        compiler_params=pltpu.CompilerParams(vmem_limit_bytes=58 * MIB),
        name="prologue",
    )(queries, key_states, value_states, tile, cell, splat_weight)


def attend_block(q_ref, group, k_s, v_s):
    low = lax.broadcasted_iota(jnp.int32, (1, LANES), 1) < HS
    q = q_ref[group, :, :LANES]
    tok, span, step = q.shape[0], k_s.shape[0], 640
    keeps = [jnp.where(low if head == 0 else ~low, 1.0, 0.0).astype(bf16) for head in range(2)]
    s = dot_nt(jnp.concatenate([q * keep for keep in keeps], axis=0), k_s[...])
    top = jnp.max(s, axis=1, keepdims=True)
    sums = [None, None]
    for begin in range(0, span, step):
        p = jnp.exp2((s[:, begin : begin + step] - top) * EXPONENT).astype(bf16)
        for head in range(2):
            term = dot(p[head * tok : (head + 1) * tok], v_s[head, begin : begin + step, :])
            sums[head] = term if sums[head] is None else sums[head] + term
    return [(head, top[head * tok : (head + 1) * tok] * EXPONENT, sums[head]) for head in range(2)]


def stage_keys(kv_ref, k_s, v_s):
    blocks, tok = kv_ref.shape[0], kv_ref.shape[1] // 2
    span = blocks * tok
    low = jnp.where(lax.broadcasted_iota(jnp.int32, (1, LANES), 1) < HS, 1.0, 0.0)
    low_b, high_b = low.astype(bf16), (1.0 - low).astype(bf16)
    k_s[...] = kv_ref[:, :tok, :].reshape(span, LANES)
    values = kv_ref[:, tok:, :].reshape(span, LANES)
    v_s[0] = values * low_b + high_b
    v_s[1] = values * high_b + low_b


def other_half(head):
    return (LANES - 1, LANES - 2) if head == 0 else (0, 1)


def first_kernel(kv_ref, q_ref, sum_ref, k_s, v_s):
    groups, tok = q_ref.shape[0], q_ref.shape[1]
    stage_keys(kv_ref, k_s, v_s)
    lane = lax.broadcasted_iota(jnp.int32, (1, LANES), 1)
    for group in range(groups):
        for head, top, sums in attend_block(q_ref, group, k_s, v_s):
            sum_ref[head, pl.ds(group * tok, tok), :] = jnp.where(lane == other_half(head)[1], top, sums)


def second_kernel(kv_ref, q_ref, sum_ref, out_ref, k_s, v_s, o_s, extra_s, slot_s, slot_t):
    groups, tok = q_ref.shape[0], q_ref.shape[1]
    tiles = out_ref.shape[0]
    slots, width = groups * SLOTS, groups * tok
    stage_keys(kv_ref, k_s, v_s)
    lane = lax.broadcasted_iota(jnp.int32, (tok, LANES), 1)
    lane_f = lane.astype(f32)
    for group in range(groups):
        rows = pl.ds(group * tok, tok)
        meta = q_ref[group, :, LANES:].astype(f32)
        tile, cell = meta[:, 0:1], meta[:, 2:3]
        place = meta[:, 1:2] + float(group * SLOTS)
        gain = meta[:, 3:4] + meta[:, 4:5]
        sums = []
        extra = jnp.where(lane_f == 96.0 + place, cell, 0.0)
        for head, top_b, sum_b in attend_block(q_ref, group, k_s, v_s):
            at, top_at = other_half(head)
            sum_a = sum_ref[head, rows, :]
            top_a = sum_a[:, top_at : top_at + 1]
            top = jnp.maximum(top_a, top_b)
            o = sum_a * jnp.exp2(top_a - top) + sum_b * jnp.exp2(top_b - top)
            total = o[:, at : at + 1]
            sums.append(o * (gain / total))
            left = top + jnp.log2(total)
            for step in range(3):
                piece = left.astype(bf16).astype(f32)
                left = left - piece
                extra = jnp.where(lane_f == step * 32.0 + head * 16.0 + place, piece, extra)
        o_s[rows, :] = jnp.where(lane < HS, sums[0], sums[1]).astype(bf16)
        extra_s[rows, :] = extra.astype(bf16)
        slot_s[rows, :] = jnp.where(lane == 0, tile * slots + place, tile * 8.0)
    slot_t[...] = jnp.transpose(slot_s[...])

    def one_hot(begin, count, at):
        row = (lax.broadcasted_iota(jnp.int32, (count, width), 0) + begin).astype(f32)
        return jnp.where(row == slot_t[at : at + 1, :], 1.0, 0.0).astype(bf16)

    step = 24
    for begin in range(0, tiles, step):
        main = dot(one_hot(begin * slots, step * slots, 0), o_s[...]).astype(bf16)
        tail = dot(one_hot(begin * 8, step * 8, 1), extra_s[...]).astype(bf16)
        out_ref[pl.ds(begin, step), :slots, :] = main.reshape(step, slots, LANES)
        out_ref[pl.ds(begin, step), slots:, :] = tail.reshape(step, 8, LANES)


def attention_cost(queries, keys):
    return pl.CostEstimate(
        flops=2 * 2 * 2 * queries * keys * LANES, bytes_accessed=4 * queries * LANES, transcendentals=2 * queries * keys
    )


def attend_first(kv, q_all):
    blocks, tok2, _ = kv.shape
    groups, tok, _ = q_all.shape
    span, rows = blocks * tok2 // 2, groups * tok
    vmem = pl.BlockSpec(memory_space=pltpu.VMEM)
    return pl.pallas_call(
        first_kernel,
        out_shape=jax.ShapeDtypeStruct((2, rows, LANES), f32),
        in_specs=[vmem, vmem],
        out_specs=vmem,
        scratch_shapes=[pltpu.VMEM((span, LANES), bf16), pltpu.VMEM((2, span, LANES), bf16)],
        compiler_params=pltpu.CompilerParams(vmem_limit_bytes=16 * MIB),
        cost_estimate=attention_cost(rows, span),
        name="attend_own_core",
    )(kv, q_all)


def attend_second(kv, q_all, sums, tiles):
    blocks, tok2, _ = kv.shape
    groups, tok, _ = q_all.shape
    span, rows = blocks * tok2 // 2, groups * tok
    vmem = pl.BlockSpec(memory_space=pltpu.VMEM)
    return pl.pallas_call(
        second_kernel,
        out_shape=jax.ShapeDtypeStruct((tiles, PIECE, LANES), bf16),
        in_specs=[vmem] * 3,
        out_specs=vmem,
        scratch_shapes=[
            pltpu.VMEM((span, LANES), bf16),
            pltpu.VMEM((2, span, LANES), bf16),
            pltpu.VMEM((rows, LANES), bf16),
            pltpu.VMEM((rows, LANES), bf16),
            pltpu.VMEM((rows, LANES), f32),
            pltpu.VMEM((LANES, rows), f32),
        ],
        compiler_params=pltpu.CompilerParams(vmem_limit_bytes=16 * MIB),
        cost_estimate=attention_cost(rows, span),
        name="attend_other_core",
    )(kv, q_all, sums)


def splat_kernel(groups, x_ref, *refs):
    out_ref, x_s, y_s, r_s = refs[-4:]
    cells = out_ref.shape[1]
    sources = x_ref.shape[0] // PIECE
    slots = groups * SLOTS
    x_s[...] = x_ref[...].astype(f32)
    meta = x_s[pl.ds(slots, sources, stride=PIECE), :]
    lse = meta + pltpu.roll(meta, LANES - 32, 1) + pltpu.roll(meta, LANES - 64, 1)
    lse = lse.reshape(sources // (2 * groups), 2 * groups, LANES)
    turns = [lse] + [pltpu.roll(lse, 2 * k, 1) for k in range(1, groups)]
    top = functools.reduce(jnp.maximum, turns)
    powers = [jnp.exp2(t - top) for t in turns]
    weight = powers[0] / functools.reduce(jnp.add, powers)
    weight = weight.reshape(sources, LANES)
    lane = lax.broadcasted_iota(jnp.int32, (sources, LANES), 1)
    y_s[...] = jnp.zeros_like(y_s)
    y_s[:sources, :] = jnp.where(lane < 32, weight, meta)
    y_t = jnp.transpose(y_s[...])
    r_s[...] = jnp.zeros_like(r_s)
    for slot in range(slots):
        r_s[pl.ds(slot * LANES, sources), :] = x_s[pl.ds(slot, sources, stride=PIECE), :].astype(bf16)
    cell = (lax.broadcasted_iota(jnp.int32, (cells, LANES), 0) + 1).astype(f32)
    hits = [cell == y_t[96 + slot : 97 + slot, :] for slot in range(slots)]
    sums = []
    for head in range(2):
        spread = jnp.concatenate(
            [
                jnp.where(hits[slot], y_t[head * 16 + slot : head * 16 + slot + 1, :], 0.0).astype(bf16)
                for slot in range(slots)
            ],
            axis=1,
        )
        sums.append(dot(spread, r_s[...]))
    low = lax.broadcasted_iota(jnp.int32, (1, LANES), 1) < HS
    features = jnp.where(low, sums[0], sums[1]).astype(bf16)
    for copy in range(out_ref.shape[0]):
        out_ref[copy] = features


def splat(received, early, cells, groups, copies):
    rows = received.shape[0]
    return pl.pallas_call(
        functools.partial(splat_kernel, groups),
        out_shape=jax.ShapeDtypeStruct((copies, cells, LANES), bf16),
        in_specs=[pl.BlockSpec(memory_space=pltpu.VMEM)] + [pl.BlockSpec(memory_space=pl.ANY)] * len(early),
        out_specs=pl.BlockSpec(memory_space=pltpu.VMEM),
        scratch_shapes=[
            pltpu.VMEM((rows, LANES), f32),
            pltpu.VMEM((LANES, LANES), f32),
            pltpu.VMEM((groups * SLOTS * LANES, LANES), bf16),
        ],
        compiler_params=pltpu.CompilerParams(vmem_limit_bytes=12 * MIB),
        name="join_splat",
    )(received, *early)


def mlp_kernel(own_ref, *refs):
    weights, (f_ref, base_hbm, gain_ref, up_ref, down_hbm) = refs[:4], refs[4:9]
    bev_ref, mix_ref, bev_s, base_s, down_s, sems = refs[9:]
    base_copy = pltpu.make_async_copy(base_hbm, base_s, sems.at[0])
    down_copy = pltpu.make_async_copy(down_hbm, down_s, sems.at[1])
    base_copy.start()
    down_copy.start()
    share = bev_ref.shape[0]
    own = own_ref[0]
    projected = None
    for k in range(0, len(weights), 2):
        features = jnp.concatenate([f_ref[own ^ k], f_ref[own ^ (k + 1)]], axis=1)
        term = dot(features, jnp.concatenate([weights[k][...], weights[k + 1][...]], axis=0))
        projected = term if projected is None else projected + term
    base_copy.wait()
    bev = base_s[...].astype(f32) + projected
    bev_s[...] = bev
    mean_square = jnp.mean(bev * bev, axis=1, keepdims=True)
    normed = (bev * lax.rsqrt(mean_square + 1e-06) * gain_ref[...]).astype(bf16)
    bev_ref[...] = bev_s[pl.ds(pl.multiple_of(own * share, share), share), :]
    step = 256
    hidden = []
    for begin in range(0, up_ref.shape[1], step):
        u = dot(normed, up_ref[:, begin : begin + step])
        hidden.append((0.5 * u * (1.0 + lax.erf(u * math.sqrt(0.5)))).astype(bf16))
    down_copy.wait()
    mixed = dot(jnp.concatenate(hidden, axis=1), down_s[...])
    mix_ref[...] = mixed.astype(bf16)


def mlp(own, weights, features, base, gain, up, down):
    heads = features.shape[0]
    cells, width = base.shape
    vmem, hbm = pl.BlockSpec(memory_space=pltpu.VMEM), pl.BlockSpec(memory_space=pltpu.HBM)
    return pl.pallas_call(
        mlp_kernel,
        out_shape=(
            jax.ShapeDtypeStruct((cells // heads, width), f32),
            jax.ShapeDtypeStruct((cells, width), bf16),
        ),
        in_specs=[pl.BlockSpec(memory_space=pltpu.SMEM)] + [vmem] * 5 + [hbm, vmem, vmem, hbm],
        out_specs=(vmem, vmem),
        scratch_shapes=[
            pltpu.VMEM((cells, width), f32),
            pltpu.VMEM((cells, width), bf16),
            pltpu.VMEM(down.shape, bf16),
            pltpu.SemaphoreType.DMA((2,)),
        ],
        compiler_params=pltpu.CompilerParams(vmem_limit_bytes=20 * MIB),
        name="project_mlp",
    )(
        own,
        *weights,
        features,
        pltpu.with_memory_space_constraint(base, pltpu.HBM),
        gain,
        up,
        pltpu.with_memory_space_constraint(down, pltpu.HBM),
    )


def swap(x, axis, bit):
    return lax.ppermute(x, axis, [(i, i ^ bit) for i in range(lax.axis_size(axis))])


def body(
    queries,
    key_states,
    value_states,
    splat_weight,
    tile_of,
    cell_of,
    bev_base,
    norm_gain,
    out_weight,
    up_weight,
    down_weight,
):
    tok = queries.shape[1]
    tiles = lax.axis_size("z") * lax.axis_size("y") * lax.axis_size("core")
    groups = lax.axis_size("y")
    heads = lax.axis_size("head")
    cells = bev_base.shape[1]
    q_copies, kv = prologue(
        queries, key_states, value_states, tile_of.reshape(1, tok), cell_of, splat_weight, groups
    )
    q_all = lax.all_to_all(q_copies, "y", 0, 0)
    own_kv = lax.all_gather(kv, "z")
    own_kv, q_all = lax.optimization_barrier((own_kv, q_all))
    other_kv = swap(own_kv, "core", 1)
    sums = attend_first(own_kv, q_all)
    packed = attend_second(other_kv, q_all, sums, tiles)
    packed, out_weight = lax.optimization_barrier((packed, out_weight))
    weights = tuple(swap(out_weight, "head", k) for k in range(heads - 1, 0, -1))[::-1]
    received = lax.all_to_all(packed, ("z", "y", "core"), 0, 0)
    features = splat(received.reshape(tiles * PIECE, LANES), weights, cells, groups, heads)
    features = lax.all_to_all(features, "head", 0, 0)
    own = lax.axis_index("head").astype(jnp.int32).reshape(1)
    bev_rows, mixed = mlp(
        own, (out_weight,) + weights, features, bev_base[0], norm_gain[None, :], up_weight, down_weight
    )
    mixed = lax.all_to_all(mixed.reshape(heads, cells // heads, mixed.shape[1]), "head", 0, 0)
    return (bev_rows + jnp.sum(mixed.astype(f32), axis=0)).astype(bf16)[None]


def solution(mesh):
    core, y = 2, 4
    z = mesh.shape["ctx"] // (core * y)
    split = Mesh(
        mesh.devices.reshape(z, y, core, mesh.shape["head"], mesh.shape["scene"]),
        ("z", "y", "core", "head", "scene"),
    )
    ctx = ("z", "y", "core")
    placed = (
        P("scene", ctx, "head"),
        P("scene", ctx, "head"),
        P("scene", ctx, "head"),
        P("scene", ctx),
        P("scene", ctx, None),
        P("scene", ctx),
        P("scene", ctx, None),
        P(),
        P("head", None),
        P(None, "head"),
        P("head", None),
    )
    return jax.shard_map(
        body,
        mesh=split,
        in_specs=placed,
        out_specs=P("scene", ctx + ("head",), None),
        check_vma=False,
    )
```

```python
import functools
import math

import jax
import jax.numpy as jnp
from jax import lax
from jax.experimental import pallas as pl
from jax.experimental.pallas import tpu as pltpu
from jax.sharding import Mesh
from jax.sharding import PartitionSpec as P

HS = 64
LANES = 128
SLOTS = 4
PIECE = 18
EXPONENT = math.log2(math.e) / math.sqrt(HS)
MIB = 1024 * 1024

f32 = jnp.float32
bf16 = jnp.bfloat16


def dot(a, b):
    return lax.dot_general(a, b, (((1,), (0,)), ((), ())), preferred_element_type=f32)


def dot_nt(a, b):
    return lax.dot_general(a, b, (((1,), (1,)), ((), ())), preferred_element_type=f32)


def prologue_kernel(q_ref, k_ref, v_ref, tile_ref, cell_ref, splat_ref, q_out, kv_out, rows_s):
    copies, tok = q_out.shape[0], q_out.shape[1]
    tile = tile_ref[...].astype(f32)
    coarse = splat_ref[...].astype(bf16).astype(f32)
    rows_s[...] = jnp.zeros_like(rows_s)
    rows_s[0:1, :tok] = tile
    rows_s[2:3, :tok] = (cell_ref[...] + 1).astype(f32)
    rows_s[3:4, :tok] = coarse
    rows_s[4:5, :tok] = splat_ref[...] - coarse
    columns = jnp.transpose(rows_s[...])[:tok, :]
    shape = (tok, tok)
    earlier = lax.broadcasted_iota(jnp.int32, shape, 1) < lax.broadcasted_iota(jnp.int32, shape, 0)
    alike = jnp.where(columns[:, 0:1] == tile, 1.0, 0.0)
    rank = jnp.sum(jnp.where(earlier, alike, 0.0), axis=1, keepdims=True)
    lane = lax.broadcasted_iota(jnp.int32, (tok, LANES), 1)
    meta = jnp.where(lane == 1, rank, columns).astype(bf16)
    for copy in range(copies):
        q_out[copy, :, :LANES] = q_ref[0]
        q_out[copy, :, LANES:] = meta
    kv_out[:tok, :] = k_ref[0]
    kv_out[tok:, :] = v_ref[0]


def prologue(queries, key_states, value_states, tile, cell, splat_weight, copies):
    tok = queries.shape[1]
    vmem = pl.BlockSpec(memory_space=pltpu.VMEM)
    return pl.pallas_call(
        prologue_kernel,
        out_shape=(
            jax.ShapeDtypeStruct((copies, tok, 2 * LANES), bf16),
            jax.ShapeDtypeStruct((2 * tok, LANES), bf16),
        ),
        in_specs=[vmem] * 6,
        out_specs=(vmem, vmem),
        scratch_shapes=[pltpu.VMEM((LANES, 2 * LANES), f32)],
        compiler_params=pltpu.CompilerParams(vmem_limit_bytes=58 * MIB),
        name="prologue",
    )(queries, key_states, value_states, tile, cell, splat_weight)


def attend_block(q_ref, group, k_s, v_s):
    low = lax.broadcasted_iota(jnp.int32, (1, LANES), 1) < HS
    q = q_ref[group, :, :LANES]
    tok, span, step = q.shape[0], k_s.shape[0], 640
    keeps = [jnp.where(low if head == 0 else ~low, 1.0, 0.0).astype(bf16) for head in range(2)]
    s = dot_nt(jnp.concatenate([q * keep for keep in keeps], axis=0), k_s[...])
    top = jnp.max(s, axis=1, keepdims=True)
    sums = [None, None]
    for begin in range(0, span, step):
        p = jnp.exp2((s[:, begin : begin + step] - top) * EXPONENT).astype(bf16)
        for head in range(2):
            term = dot(p[head * tok : (head + 1) * tok], v_s[head, begin : begin + step, :])
            sums[head] = term if sums[head] is None else sums[head] + term
    return [(head, top[head * tok : (head + 1) * tok] * EXPONENT, sums[head]) for head in range(2)]


def stage_keys(kv_ref, k_s, v_s):
    blocks, tok = kv_ref.shape[0], kv_ref.shape[1] // 2
    span = blocks * tok
    low = jnp.where(lax.broadcasted_iota(jnp.int32, (1, LANES), 1) < HS, 1.0, 0.0)
    low_b, high_b = low.astype(bf16), (1.0 - low).astype(bf16)
    k_s[...] = kv_ref[:, :tok, :].reshape(span, LANES)
    values = kv_ref[:, tok:, :].reshape(span, LANES)
    v_s[0] = values * low_b + high_b
    v_s[1] = values * high_b + low_b


def other_half(head):
    return (LANES - 1, LANES - 2) if head == 0 else (0, 1)


def first_kernel(kv_ref, q_ref, sum_ref, k_s, v_s):
    groups, tok = q_ref.shape[0], q_ref.shape[1]
    stage_keys(kv_ref, k_s, v_s)
    lane = lax.broadcasted_iota(jnp.int32, (1, LANES), 1)
    for group in range(groups):
        for head, top, sums in attend_block(q_ref, group, k_s, v_s):
            sum_ref[head, pl.ds(group * tok, tok), :] = jnp.where(lane == other_half(head)[1], top, sums)


def second_kernel(kv_ref, q_ref, sum_ref, out_ref, k_s, v_s, o_s, extra_s, slot_s, slot_t):
    groups, tok = q_ref.shape[0], q_ref.shape[1]
    slots, width = groups * SLOTS, groups * tok
    stage_keys(kv_ref, k_s, v_s)
    lane = lax.broadcasted_iota(jnp.int32, (tok, LANES), 1)
    lane_f = lane.astype(f32)
    for group in range(groups):
        rows = pl.ds(group * tok, tok)
        meta = q_ref[group, :, LANES:].astype(f32)
        tile, cell = meta[:, 0:1], meta[:, 2:3]
        place = meta[:, 1:2] + float(group * SLOTS)
        gain = meta[:, 3:4] + meta[:, 4:5]
        sums = []
        extra = jnp.where(lane_f == 96.0 + place, cell, 0.0)
        for head, top_b, sum_b in attend_block(q_ref, group, k_s, v_s):
            at, top_at = other_half(head)
            sum_a = sum_ref[head, rows, :]
            top_a = sum_a[:, top_at : top_at + 1]
            top = jnp.maximum(top_a, top_b)
            o = sum_a * jnp.exp2(top_a - top) + sum_b * jnp.exp2(top_b - top)
            total = o[:, at : at + 1]
            sums.append(o * (gain / total))
            left = top + jnp.log2(total)
            for step in range(3):
                piece = left.astype(bf16).astype(f32)
                left = left - piece
                extra = jnp.where(lane_f == step * 32.0 + head * 16.0 + place, piece, extra)
        o_s[rows, :] = jnp.where(lane < HS, sums[0], sums[1]).astype(bf16)
        extra_s[rows, :] = extra.astype(bf16)
        slot_s[rows, :] = tile * PIECE + jnp.where(lane == 0, place, float(slots))
    slot_t[...] = jnp.transpose(slot_s[...])
    step = 16 * PIECE
    for begin in range(0, out_ref.shape[0], step):
        row = (lax.broadcasted_iota(jnp.int32, (step, width), 0) + begin).astype(f32)
        main = jnp.where(row == slot_t[0:1, :], 1.0, 0.0).astype(bf16)
        tail = jnp.where(row == slot_t[1:2, :], 1.0, 0.0).astype(bf16)
        out_ref[pl.ds(begin, step), :] = (dot(main, o_s[...]) + dot(tail, extra_s[...])).astype(bf16)


def attention_cost(queries, keys):
    return pl.CostEstimate(
        flops=2 * 2 * 2 * queries * keys * LANES, bytes_accessed=4 * queries * LANES, transcendentals=2 * queries * keys
    )


def attend_first(kv, q_all):
    blocks, tok2, _ = kv.shape
    groups, tok, _ = q_all.shape
    span, rows = blocks * tok2 // 2, groups * tok
    vmem = pl.BlockSpec(memory_space=pltpu.VMEM)
    return pl.pallas_call(
        first_kernel,
        out_shape=jax.ShapeDtypeStruct((2, rows, LANES), f32),
        in_specs=[vmem, vmem],
        out_specs=vmem,
        scratch_shapes=[pltpu.VMEM((span, LANES), bf16), pltpu.VMEM((2, span, LANES), bf16)],
        compiler_params=pltpu.CompilerParams(vmem_limit_bytes=16 * MIB),
        cost_estimate=attention_cost(rows, span),
        name="attend_own_core",
    )(kv, q_all)


def attend_second(kv, q_all, sums, tiles):
    blocks, tok2, _ = kv.shape
    groups, tok, _ = q_all.shape
    span, rows = blocks * tok2 // 2, groups * tok
    vmem = pl.BlockSpec(memory_space=pltpu.VMEM)
    return pl.pallas_call(
        second_kernel,
        out_shape=jax.ShapeDtypeStruct((tiles * PIECE, LANES), bf16),
        in_specs=[vmem] * 3,
        out_specs=vmem,
        scratch_shapes=[
            pltpu.VMEM((span, LANES), bf16),
            pltpu.VMEM((2, span, LANES), bf16),
            pltpu.VMEM((rows, LANES), bf16),
            pltpu.VMEM((rows, LANES), bf16),
            pltpu.VMEM((rows, LANES), f32),
            pltpu.VMEM((LANES, rows), f32),
        ],
        compiler_params=pltpu.CompilerParams(vmem_limit_bytes=16 * MIB),
        cost_estimate=attention_cost(rows, span),
        name="attend_other_core",
    )(kv, q_all, sums)


def splat_kernel(groups, x_ref, *refs):
    out_ref, x_s, y_s, r_s = refs[-4:]
    cells = out_ref.shape[1]
    sources = x_ref.shape[0] // PIECE
    slots = groups * SLOTS
    x_s[...] = x_ref[...].astype(f32)
    meta = x_s[pl.ds(slots, sources, stride=PIECE), :]
    lse = meta + pltpu.roll(meta, LANES - 32, 1) + pltpu.roll(meta, LANES - 64, 1)
    lse = lse.reshape(sources // (2 * groups), 2 * groups, LANES)
    turns = [lse] + [pltpu.roll(lse, 2 * k, 1) for k in range(1, groups)]
    top = functools.reduce(jnp.maximum, turns)
    powers = [jnp.exp2(t - top) for t in turns]
    weight = powers[0] / functools.reduce(jnp.add, powers)
    weight = weight.reshape(sources, LANES)
    lane = lax.broadcasted_iota(jnp.int32, (sources, LANES), 1)
    y_s[...] = jnp.zeros_like(y_s)
    y_s[:sources, :] = jnp.where(lane < 32, weight, meta)
    y_t = jnp.transpose(y_s[...])
    r_s[...] = jnp.zeros_like(r_s)
    for slot in range(slots):
        r_s[pl.ds(slot * LANES, sources), :] = x_s[pl.ds(slot, sources, stride=PIECE), :].astype(bf16)
    cell = (lax.broadcasted_iota(jnp.int32, (cells, LANES), 0) + 1).astype(f32)
    hits = [cell == y_t[96 + slot : 97 + slot, :] for slot in range(slots)]
    sums = []
    for head in range(2):
        spread = jnp.concatenate(
            [
                jnp.where(hits[slot], y_t[head * 16 + slot : head * 16 + slot + 1, :], 0.0).astype(bf16)
                for slot in range(slots)
            ],
            axis=1,
        )
        sums.append(dot(spread, r_s[...]))
    low = lax.broadcasted_iota(jnp.int32, (1, LANES), 1) < HS
    features = jnp.where(low, sums[0], sums[1]).astype(bf16)
    for copy in range(out_ref.shape[0]):
        out_ref[copy] = features


def splat(received, early, cells, groups, copies):
    rows = received.shape[0]
    return pl.pallas_call(
        functools.partial(splat_kernel, groups),
        out_shape=jax.ShapeDtypeStruct((copies, cells, LANES), bf16),
        in_specs=[pl.BlockSpec(memory_space=pltpu.VMEM)] + [pl.BlockSpec(memory_space=pl.ANY)] * len(early),
        out_specs=pl.BlockSpec(memory_space=pltpu.VMEM),
        scratch_shapes=[
            pltpu.VMEM((rows, LANES), f32),
            pltpu.VMEM((LANES, LANES), f32),
            pltpu.VMEM((groups * SLOTS * LANES, LANES), bf16),
        ],
        compiler_params=pltpu.CompilerParams(vmem_limit_bytes=12 * MIB),
        name="join_splat",
    )(received, *early)


def mlp_kernel(own_ref, *refs):
    weights, (f_ref, base_hbm, gain_ref, up_ref, down_hbm) = refs[:4], refs[4:9]
    bev_ref, mix_ref, bev_s, base_s, down_s, sems = refs[9:]
    base_copy = pltpu.make_async_copy(base_hbm, base_s, sems.at[0])
    down_copy = pltpu.make_async_copy(down_hbm, down_s, sems.at[1])
    base_copy.start()
    share = bev_ref.shape[0]
    own = own_ref[0]
    projected = None
    for k in range(0, len(weights), 2):
        features = jnp.concatenate([f_ref[own ^ k], f_ref[own ^ (k + 1)]], axis=1)
        term = dot(features, jnp.concatenate([weights[k][...], weights[k + 1][...]], axis=0))
        projected = term if projected is None else projected + term
    base_copy.wait()
    down_copy.start()
    bev = base_s[...].astype(f32) + projected
    bev_s[...] = bev
    mean_square = jnp.mean(bev * bev, axis=1, keepdims=True)
    normed = (bev * lax.rsqrt(mean_square + 1e-06) * gain_ref[...]).astype(bf16)
    bev_ref[...] = bev_s[pl.ds(pl.multiple_of(own * share, share), share), :]
    step = 256
    hidden = []
    for begin in range(0, up_ref.shape[1], step):
        u = dot(normed, up_ref[:, begin : begin + step])
        hidden.append((0.5 * u * (1.0 + lax.erf(u * math.sqrt(0.5)))).astype(bf16))
    down_copy.wait()
    mixed = dot(jnp.concatenate(hidden, axis=1), down_s[...])
    mix_ref[...] = mixed.astype(bf16)


def mlp(own, weights, features, base, gain, up, down):
    heads = features.shape[0]
    cells, width = base.shape
    vmem, hbm = pl.BlockSpec(memory_space=pltpu.VMEM), pl.BlockSpec(memory_space=pltpu.HBM)
    return pl.pallas_call(
        mlp_kernel,
        out_shape=(
            jax.ShapeDtypeStruct((cells // heads, width), f32),
            jax.ShapeDtypeStruct((cells, width), bf16),
        ),
        in_specs=[pl.BlockSpec(memory_space=pltpu.SMEM)] + [vmem] * 5 + [hbm, vmem, vmem, hbm],
        out_specs=(vmem, vmem),
        scratch_shapes=[
            pltpu.VMEM((cells, width), f32),
            pltpu.VMEM((cells, width), bf16),
            pltpu.VMEM(down.shape, bf16),
            pltpu.SemaphoreType.DMA((2,)),
        ],
        compiler_params=pltpu.CompilerParams(vmem_limit_bytes=20 * MIB),
        name="project_mlp",
    )(
        own,
        *weights,
        features,
        pltpu.with_memory_space_constraint(base, pltpu.HBM),
        gain,
        up,
        pltpu.with_memory_space_constraint(down, pltpu.HBM),
    )


def swap(x, axis, bit):
    return lax.ppermute(x, axis, [(i, i ^ bit) for i in range(lax.axis_size(axis))])


def body(
    queries,
    key_states,
    value_states,
    splat_weight,
    tile_of,
    cell_of,
    bev_base,
    norm_gain,
    out_weight,
    up_weight,
    down_weight,
):
    tok = queries.shape[1]
    tiles = lax.axis_size("z") * lax.axis_size("y") * lax.axis_size("core")
    groups = lax.axis_size("y")
    heads = lax.axis_size("head")
    cells = bev_base.shape[1]
    q_copies, kv = prologue(
        queries, key_states, value_states, tile_of.reshape(1, tok), cell_of, splat_weight, groups
    )
    q_all = lax.all_to_all(q_copies, "y", 0, 0)
    own_kv = lax.all_gather(kv, "z")
    own_kv, q_all = lax.optimization_barrier((own_kv, q_all))
    other_kv = swap(own_kv, "core", 1)
    sums = attend_first(own_kv, q_all)
    packed = attend_second(other_kv, q_all, sums, tiles)
    packed, out_weight = lax.optimization_barrier((packed, out_weight))
    weights = tuple(swap(out_weight, "head", k) for k in range(heads - 1, 0, -1))[::-1]
    received = lax.all_to_all(packed.reshape(tiles, PIECE // 2, 2, LANES), ("z", "y", "core"), 0, 0)
    features = splat(received.reshape(tiles * PIECE, LANES), weights, cells, groups, heads)
    features = lax.all_to_all(features, "head", 0, 0)
    own = lax.axis_index("head").astype(jnp.int32).reshape(1)
    bev_rows, mixed = mlp(
        own, (out_weight,) + weights, features, bev_base[0], norm_gain[None, :], up_weight, down_weight
    )
    mixed = lax.all_to_all(mixed.reshape(heads, cells // heads, mixed.shape[1]), "head", 0, 0)
    return (bev_rows + jnp.sum(mixed.astype(f32), axis=0)).astype(bf16)[None]


def solution(mesh):
    core, y = 2, 4
    z = mesh.shape["ctx"] // (core * y)
    split = Mesh(
        mesh.devices.reshape(z, y, core, mesh.shape["head"], mesh.shape["scene"]),
        ("z", "y", "core", "head", "scene"),
    )
    ctx = ("z", "y", "core")
    placed = (
        P("scene", ctx, "head"),
        P("scene", ctx, "head"),
        P("scene", ctx, "head"),
        P("scene", ctx),
        P("scene", ctx, None),
        P("scene", ctx),
        P("scene", ctx, None),
        P(),
        P("head", None),
        P(None, "head"),
        P("head", None),
    )
    return jax.shard_map(
        body,
        mesh=split,
        in_specs=placed,
        out_specs=P("scene", ctx + ("head",), None),
        check_vma=False,
    )
```

```python
import functools
import math

import jax
import jax.numpy as jnp
from jax import lax
from jax.experimental import pallas as pl
from jax.experimental.pallas import tpu as pltpu
from jax.sharding import Mesh
from jax.sharding import PartitionSpec as P

HS = 64
LANES = 128
SLOTS = 4
PIECE = 18
EXPONENT = math.log2(math.e) / math.sqrt(HS)
MIB = 1024 * 1024
MLP_STEPS = 2

f32 = jnp.float32
bf16 = jnp.bfloat16


def dot(a, b):
    return lax.dot_general(a, b, (((1,), (0,)), ((), ())), preferred_element_type=f32)


def dot_nt(a, b):
    return lax.dot_general(a, b, (((1,), (1,)), ((), ())), preferred_element_type=f32)


def prologue_kernel(q_ref, k_ref, v_ref, tile_ref, cell_ref, splat_ref, q_out, kv_out, rows_s):
    copies, tok = q_out.shape[0], q_out.shape[1]
    tile = tile_ref[...].astype(f32)
    coarse = splat_ref[...].astype(bf16).astype(f32)
    rows_s[...] = jnp.zeros_like(rows_s)
    rows_s[0:1, :tok] = tile
    rows_s[2:3, :tok] = (cell_ref[...] + 1).astype(f32)
    rows_s[3:4, :tok] = coarse
    rows_s[4:5, :tok] = splat_ref[...] - coarse
    columns = jnp.transpose(rows_s[...])[:tok, :]
    shape = (tok, tok)
    earlier = lax.broadcasted_iota(jnp.int32, shape, 1) < lax.broadcasted_iota(jnp.int32, shape, 0)
    alike = jnp.where(columns[:, 0:1] == tile, 1.0, 0.0)
    rank = jnp.sum(jnp.where(earlier, alike, 0.0), axis=1, keepdims=True)
    lane = lax.broadcasted_iota(jnp.int32, (tok, LANES), 1)
    meta = jnp.where(lane == 1, rank, columns).astype(bf16)
    for copy in range(copies):
        q_out[copy, :, :LANES] = q_ref[0]
        q_out[copy, :, LANES:] = meta
    kv_out[:tok, :] = k_ref[0]
    kv_out[tok:, :] = v_ref[0]


def prologue(queries, key_states, value_states, tile, cell, splat_weight, copies):
    tok = queries.shape[1]
    vmem = pl.BlockSpec(memory_space=pltpu.VMEM)
    return pl.pallas_call(
        prologue_kernel,
        out_shape=(
            jax.ShapeDtypeStruct((copies, tok, 2 * LANES), bf16),
            jax.ShapeDtypeStruct((2 * tok, LANES), bf16),
        ),
        in_specs=[vmem] * 6,
        out_specs=(vmem, vmem),
        scratch_shapes=[pltpu.VMEM((LANES, 2 * LANES), f32)],
        compiler_params=pltpu.CompilerParams(vmem_limit_bytes=58 * MIB),
        name="prologue",
    )(queries, key_states, value_states, tile, cell, splat_weight)


def attend_blocks(q_ref, first, count, k_s, v_s):
    low = lax.broadcasted_iota(jnp.int32, (1, LANES), 1) < HS
    q = jnp.concatenate([q_ref[first + i, :, :LANES] for i in range(count)], axis=0)
    rows, span, step = q.shape[0], k_s.shape[0], 640
    keeps = [jnp.where(low if head == 0 else ~low, 1.0, 0.0).astype(bf16) for head in range(2)]
    s = dot_nt(jnp.concatenate([q * keep for keep in keeps], axis=0), k_s[...])
    top = jnp.max(s, axis=1, keepdims=True)
    sums = [None, None]
    for begin in range(0, span, step):
        p = jnp.exp2((s[:, begin : begin + step] - top) * EXPONENT).astype(bf16)
        for head in range(2):
            term = dot(p[head * rows : (head + 1) * rows], v_s[head, begin : begin + step, :])
            sums[head] = term if sums[head] is None else sums[head] + term
    return [(head, top[head * rows : (head + 1) * rows] * EXPONENT, sums[head]) for head in range(2)]


def stage_keys(kv_ref, k_s, v_s):
    blocks, tok = kv_ref.shape[0], kv_ref.shape[1] // 2
    span = blocks * tok
    low = jnp.where(lax.broadcasted_iota(jnp.int32, (1, LANES), 1) < HS, 1.0, 0.0)
    low_b, high_b = low.astype(bf16), (1.0 - low).astype(bf16)
    k_s[...] = kv_ref[:, :tok, :].reshape(span, LANES)
    values = kv_ref[:, tok:, :].reshape(span, LANES)
    v_s[0] = values * low_b + high_b
    v_s[1] = values * high_b + low_b


def other_half(head):
    return (LANES - 1, LANES - 2) if head == 0 else (0, 1)


def first_kernel(kv_ref, q_ref, sum_ref, k_s, v_s):
    groups, tok = q_ref.shape[0], q_ref.shape[1]
    stage_keys(kv_ref, k_s, v_s)
    lane = lax.broadcasted_iota(jnp.int32, (1, LANES), 1)
    for group in range(0, groups, 2):
        for head, top, sums in attend_blocks(q_ref, group, 2, k_s, v_s):
            sum_ref[head, pl.ds(group * tok, 2 * tok), :] = jnp.where(lane == other_half(head)[1], top, sums)


def second_kernel(kv_ref, q_ref, sum_ref, out_ref, k_s, v_s, o_s, extra_s, slot_s, slot_t, packed_s):
    groups, tok = q_ref.shape[0], q_ref.shape[1]
    slots, width = groups * SLOTS, groups * tok
    stage_keys(kv_ref, k_s, v_s)
    lane = lax.broadcasted_iota(jnp.int32, (tok, LANES), 1)
    lane_f = lane.astype(f32)
    for group in range(groups):
        rows = pl.ds(group * tok, tok)
        meta = q_ref[group, :, LANES:].astype(f32)
        tile, cell = meta[:, 0:1], meta[:, 2:3]
        place = meta[:, 1:2] + float(group * SLOTS)
        gain = meta[:, 3:4] + meta[:, 4:5]
        sums = []
        extra = jnp.where(lane_f == 96.0 + place, cell, 0.0)
        for head, top_b, sum_b in attend_blocks(q_ref, group, 1, k_s, v_s):
            at, top_at = other_half(head)
            sum_a = sum_ref[head, rows, :]
            top_a = sum_a[:, top_at : top_at + 1]
            top = jnp.maximum(top_a, top_b)
            o = sum_a * jnp.exp2(top_a - top) + sum_b * jnp.exp2(top_b - top)
            total = o[:, at : at + 1]
            sums.append(o * (gain / total))
            left = top + jnp.log2(total)
            for step in range(3):
                piece = left.astype(bf16).astype(f32)
                left = left - piece
                extra = jnp.where(lane_f == step * 32.0 + head * 16.0 + place, piece, extra)
        o_s[rows, :] = jnp.where(lane < HS, sums[0], sums[1]).astype(bf16)
        extra_s[rows, :] = extra.astype(bf16)
        slot_s[rows, :] = jnp.where(lane == 0, tile * PIECE + place, tile)
    slot_t[...] = jnp.transpose(slot_s[...])
    step = 16 * PIECE
    tiles = out_ref.shape[0] // PIECE
    for begin in range(0, out_ref.shape[0], step):
        row = (lax.broadcasted_iota(jnp.int32, (step, width), 0) + begin).astype(f32)
        main = jnp.where(row == slot_t[0:1, :], 1.0, 0.0).astype(bf16)
        packed_s[pl.ds(begin, step), :] = dot(main, o_s[...])
    row = lax.broadcasted_iota(jnp.int32, (tiles, width), 0).astype(f32)
    tail = jnp.where(row == slot_t[1:2, :], 1.0, 0.0).astype(bf16)
    packed_s[pl.ds(slots, tiles, stride=PIECE), :] = dot(tail, extra_s[...])
    out_ref[...] = packed_s[...].astype(bf16)


def attention_cost(queries, keys):
    return pl.CostEstimate(
        flops=2 * 2 * 2 * queries * keys * LANES, bytes_accessed=4 * queries * LANES, transcendentals=2 * queries * keys
    )


def attend_first(kv, q_all):
    blocks, tok2, _ = kv.shape
    groups, tok, _ = q_all.shape
    span, rows = blocks * tok2 // 2, groups * tok
    vmem = pl.BlockSpec(memory_space=pltpu.VMEM)
    return pl.pallas_call(
        first_kernel,
        out_shape=jax.ShapeDtypeStruct((2, rows, LANES), f32),
        in_specs=[vmem, vmem],
        out_specs=vmem,
        scratch_shapes=[pltpu.VMEM((span, LANES), bf16), pltpu.VMEM((2, span, LANES), bf16)],
        compiler_params=pltpu.CompilerParams(vmem_limit_bytes=16 * MIB),
        cost_estimate=attention_cost(rows, span),
        name="attend_own_core",
    )(kv, q_all)


def attend_second(kv, q_all, sums, tiles):
    blocks, tok2, _ = kv.shape
    groups, tok, _ = q_all.shape
    span, rows = blocks * tok2 // 2, groups * tok
    vmem = pl.BlockSpec(memory_space=pltpu.VMEM)
    return pl.pallas_call(
        second_kernel,
        out_shape=jax.ShapeDtypeStruct((tiles * PIECE, LANES), bf16),
        in_specs=[vmem] * 3,
        out_specs=vmem,
        scratch_shapes=[
            pltpu.VMEM((span, LANES), bf16),
            pltpu.VMEM((2, span, LANES), bf16),
            pltpu.VMEM((rows, LANES), bf16),
            pltpu.VMEM((rows, LANES), bf16),
            pltpu.VMEM((rows, LANES), f32),
            pltpu.VMEM((LANES, rows), f32),
            pltpu.VMEM((tiles * PIECE, LANES), f32),
        ],
        compiler_params=pltpu.CompilerParams(vmem_limit_bytes=16 * MIB),
        cost_estimate=attention_cost(rows, span),
        name="attend_other_core",
    )(kv, q_all, sums)


def splat_kernel(groups, x_ref, *refs):
    out_ref, x_s, y_s, r_s = refs[-4:]
    cells = out_ref.shape[1]
    sources = x_ref.shape[0] // PIECE
    slots = groups * SLOTS
    x_s[...] = x_ref[...].astype(f32)
    meta = x_s[pl.ds(slots, sources, stride=PIECE), :]
    lse = meta + pltpu.roll(meta, LANES - 32, 1) + pltpu.roll(meta, LANES - 64, 1)
    lse = lse.reshape(sources // (2 * groups), 2 * groups, LANES)
    turns = [lse] + [pltpu.roll(lse, 2 * k, 1) for k in range(1, groups)]
    top = functools.reduce(jnp.maximum, turns)
    powers = [jnp.exp2(t - top) for t in turns]
    weight = powers[0] / functools.reduce(jnp.add, powers)
    weight = weight.reshape(sources, LANES)
    lane = lax.broadcasted_iota(jnp.int32, (sources, LANES), 1)
    y_s[...] = jnp.zeros_like(y_s)
    y_s[:sources, :] = jnp.where(lane < 32, weight, meta)
    y_t = jnp.transpose(y_s[...])
    r_s[...] = jnp.zeros_like(r_s)
    for slot in range(slots):
        r_s[pl.ds(slot * LANES, sources), :] = x_s[pl.ds(slot, sources, stride=PIECE), :].astype(bf16)
    cell = (lax.broadcasted_iota(jnp.int32, (cells, LANES), 0) + 1).astype(f32)
    hits = [cell == y_t[96 + slot : 97 + slot, :] for slot in range(slots)]
    sums = []
    for head in range(2):
        spread = jnp.concatenate(
            [
                jnp.where(hits[slot], y_t[head * 16 + slot : head * 16 + slot + 1, :], 0.0).astype(bf16)
                for slot in range(slots)
            ],
            axis=1,
        )
        sums.append(dot(spread, r_s[...]))
    low = lax.broadcasted_iota(jnp.int32, (1, LANES), 1) < HS
    features = jnp.where(low, sums[0], sums[1]).astype(bf16)
    for copy in range(out_ref.shape[0]):
        out_ref[copy] = features


def splat(received, early, cells, groups, copies):
    rows = received.shape[0]
    return pl.pallas_call(
        functools.partial(splat_kernel, groups),
        out_shape=jax.ShapeDtypeStruct((copies, cells, LANES), bf16),
        in_specs=[pl.BlockSpec(memory_space=pltpu.VMEM)] + [pl.BlockSpec(memory_space=pl.ANY)] * len(early),
        out_specs=pl.BlockSpec(memory_space=pltpu.VMEM),
        scratch_shapes=[
            pltpu.VMEM((rows, LANES), f32),
            pltpu.VMEM((LANES, LANES), f32),
            pltpu.VMEM((groups * SLOTS * LANES, LANES), bf16),
        ],
        compiler_params=pltpu.CompilerParams(vmem_limit_bytes=12 * MIB),
        name="join_splat",
    )(received, *early)


def mlp_kernel(own_ref, *refs):
    weights, (f_ref, base_hbm, gain_ref, up_ref, down_hbm) = refs[:4], refs[4:9]
    bev_ref, mix_ref, bev_s, base_s, down_s, sems = refs[9:]
    base_copy = pltpu.make_async_copy(base_hbm, base_s, sems.at[0])
    down_copy = pltpu.make_async_copy(down_hbm, down_s, sems.at[1])
    base_copy.start()
    down_copy.start()
    share = bev_ref.shape[0]
    own = own_ref[0]
    projected = None
    for k in range(0, len(weights), 2):
        features = jnp.concatenate([f_ref[own ^ k], f_ref[own ^ (k + 1)]], axis=1)
        term = dot(features, jnp.concatenate([weights[k][...], weights[k + 1][...]], axis=0))
        projected = term if projected is None else projected + term
    base_copy.wait()
    bev = base_s[...].astype(f32) + projected
    bev_s[...] = bev
    mean_square = jnp.mean(bev * bev, axis=1, keepdims=True)
    normed = (bev * lax.rsqrt(mean_square + 1e-06) * gain_ref[...]).astype(bf16)
    bev_ref[...] = bev_s[pl.ds(pl.multiple_of(own * share, share), share), :]
    step = up_ref.shape[1] // MLP_STEPS
    mixed = None
    for begin in range(0, up_ref.shape[1], step):
        u = dot(normed, up_ref[:, begin : begin + step])
        hidden = (0.5 * u * (1.0 + lax.erf(u * math.sqrt(0.5)))).astype(bf16)
        if begin == 0:
            down_copy.wait()
        term = dot(hidden, down_s[begin : begin + step, :])
        mixed = term if mixed is None else mixed + term
    mix_ref[...] = mixed.astype(bf16)


def mlp(own, weights, features, base, gain, up, down):
    heads = features.shape[0]
    cells, width = base.shape
    vmem, hbm = pl.BlockSpec(memory_space=pltpu.VMEM), pl.BlockSpec(memory_space=pltpu.HBM)
    return pl.pallas_call(
        mlp_kernel,
        out_shape=(
            jax.ShapeDtypeStruct((cells // heads, width), f32),
            jax.ShapeDtypeStruct((cells, width), bf16),
        ),
        in_specs=[pl.BlockSpec(memory_space=pltpu.SMEM)] + [vmem] * 5 + [hbm, vmem, vmem, hbm],
        out_specs=(vmem, vmem),
        scratch_shapes=[
            pltpu.VMEM((cells, width), f32),
            pltpu.VMEM((cells, width), bf16),
            pltpu.VMEM(down.shape, bf16),
            pltpu.SemaphoreType.DMA((2,)),
        ],
        compiler_params=pltpu.CompilerParams(vmem_limit_bytes=20 * MIB),
        name="project_mlp",
    )(
        own,
        *weights,
        features,
        pltpu.with_memory_space_constraint(base, pltpu.HBM),
        gain,
        up,
        pltpu.with_memory_space_constraint(down, pltpu.HBM),
    )


def swap(x, axis, bit):
    return lax.ppermute(x, axis, [(i, i ^ bit) for i in range(lax.axis_size(axis))])


def body(
    queries,
    key_states,
    value_states,
    splat_weight,
    tile_of,
    cell_of,
    bev_base,
    norm_gain,
    out_weight,
    up_weight,
    down_weight,
):
    tok = queries.shape[1]
    tiles = lax.axis_size("z") * lax.axis_size("y") * lax.axis_size("core")
    groups = lax.axis_size("y")
    heads = lax.axis_size("head")
    cells = bev_base.shape[1]
    q_copies, kv = prologue(
        queries, key_states, value_states, tile_of.reshape(1, tok), cell_of, splat_weight, groups
    )
    q_all = lax.all_to_all(q_copies, "y", 0, 0)
    own_kv = lax.all_gather(kv, "z")
    own_kv, q_all = lax.optimization_barrier((own_kv, q_all))
    other_kv = swap(own_kv, "core", 1)
    sums = attend_first(own_kv, q_all)
    packed = attend_second(other_kv, q_all, sums, tiles)
    packed, out_weight = lax.optimization_barrier((packed, out_weight))
    weights = tuple(swap(out_weight, "head", k) for k in range(heads - 1, 0, -1))[::-1]
    received = lax.all_to_all(packed.reshape(tiles, PIECE // 2, 2, LANES), ("z", "y", "core"), 0, 0)
    features = splat(received.reshape(tiles * PIECE, LANES), weights, cells, groups, heads)
    features = lax.all_to_all(features, "head", 0, 0)
    own = lax.axis_index("head").astype(jnp.int32).reshape(1)
    bev_rows, mixed = mlp(
        own, (out_weight,) + weights, features, bev_base[0], norm_gain[None, :], up_weight, down_weight
    )
    mixed = lax.all_to_all(mixed.reshape(heads, cells // heads, mixed.shape[1]), "head", 0, 0)
    return (bev_rows + jnp.sum(mixed.astype(f32), axis=0)).astype(bf16)[None]


def solution(mesh):
    core, y = 2, 4
    z = mesh.shape["ctx"] // (core * y)
    split = Mesh(
        mesh.devices.reshape(z, y, core, mesh.shape["head"], mesh.shape["scene"]),
        ("z", "y", "core", "head", "scene"),
    )
    ctx = ("z", "y", "core")
    placed = (
        P("scene", ctx, "head"),
        P("scene", ctx, "head"),
        P("scene", ctx, "head"),
        P("scene", ctx),
        P("scene", ctx, None),
        P("scene", ctx),
        P("scene", ctx, None),
        P(),
        P("head", None),
        P(None, "head"),
        P("head", None),
    )
    return jax.shard_map(
        body,
        mesh=split,
        in_specs=placed,
        out_specs=P("scene", ctx + ("head",), None),
        check_vma=False,
    )
```

```python
import functools
import math

import jax
import jax.numpy as jnp
from jax import lax
from jax.experimental import pallas as pl
from jax.experimental.pallas import tpu as pltpu
from jax.sharding import Mesh
from jax.sharding import PartitionSpec as P

HS = 64
LANES = 128
SLOTS = 4
PIECE = 18
EXPONENT = math.log2(math.e) / math.sqrt(HS)
MIB = 1024 * 1024
MLP_STEPS = 2

f32 = jnp.float32
bf16 = jnp.bfloat16


def dot(a, b):
    return lax.dot_general(a, b, (((1,), (0,)), ((), ())), preferred_element_type=f32)


def dot_nt(a, b):
    return lax.dot_general(a, b, (((1,), (1,)), ((), ())), preferred_element_type=f32)


def prologue_kernel(q_ref, k_ref, v_ref, tile_ref, cell_ref, splat_ref, q_out, kv_out, rows_s):
    copies, tok = q_out.shape[0], q_out.shape[1]
    tile = tile_ref[...].astype(f32)
    coarse = splat_ref[...].astype(bf16).astype(f32)
    rows_s[...] = jnp.zeros_like(rows_s)
    rows_s[0:1, :tok] = tile
    rows_s[2:3, :tok] = (cell_ref[...] + 1).astype(f32)
    rows_s[3:4, :tok] = coarse
    rows_s[4:5, :tok] = splat_ref[...] - coarse
    columns = jnp.transpose(rows_s[...])[:tok, :]
    shape = (tok, tok)
    earlier = lax.broadcasted_iota(jnp.int32, shape, 1) < lax.broadcasted_iota(jnp.int32, shape, 0)
    alike = jnp.where(columns[:, 0:1] == tile, 1.0, 0.0)
    rank = jnp.sum(jnp.where(earlier, alike, 0.0), axis=1, keepdims=True)
    lane = lax.broadcasted_iota(jnp.int32, (tok, LANES), 1)
    meta = jnp.where(lane == 1, rank, columns).astype(bf16)
    for copy in range(copies):
        q_out[copy, :, :LANES] = q_ref[0]
        q_out[copy, :, LANES:] = meta
    kv_out[:tok, :] = k_ref[0]
    kv_out[tok:, :] = v_ref[0]


def prologue(queries, key_states, value_states, tile, cell, splat_weight, copies):
    tok = queries.shape[1]
    vmem = pl.BlockSpec(memory_space=pltpu.VMEM)
    return pl.pallas_call(
        prologue_kernel,
        out_shape=(
            jax.ShapeDtypeStruct((copies, tok, 2 * LANES), bf16),
            jax.ShapeDtypeStruct((2 * tok, LANES), bf16),
        ),
        in_specs=[vmem] * 6,
        out_specs=(vmem, vmem),
        scratch_shapes=[pltpu.VMEM((LANES, 2 * LANES), f32)],
        compiler_params=pltpu.CompilerParams(vmem_limit_bytes=58 * MIB),
        name="prologue",
    )(queries, key_states, value_states, tile, cell, splat_weight)


def attend_blocks(q_ref, first, count, k_s, v_s):
    low = lax.broadcasted_iota(jnp.int32, (1, LANES), 1) < HS
    q = jnp.concatenate([q_ref[first + i, :, :LANES] for i in range(count)], axis=0)
    rows, span, step = q.shape[0], k_s.shape[0], 640
    keeps = [jnp.where(low if head == 0 else ~low, 1.0, 0.0).astype(bf16) for head in range(2)]
    s = dot_nt(jnp.concatenate([q * keep for keep in keeps], axis=0), k_s[...])
    top = jnp.max(s, axis=1, keepdims=True)
    sums = [None, None]
    for begin in range(0, span, step):
        p = jnp.exp2((s[:, begin : begin + step] - top) * EXPONENT).astype(bf16)
        for head in range(2):
            term = dot(p[head * rows : (head + 1) * rows], v_s[head, begin : begin + step, :])
            sums[head] = term if sums[head] is None else sums[head] + term
    return [(head, top[head * rows : (head + 1) * rows] * EXPONENT, sums[head]) for head in range(2)]


def stage_keys(kv_ref, k_s, v_s):
    blocks, tok = kv_ref.shape[0], kv_ref.shape[1] // 2
    span = blocks * tok
    low = jnp.where(lax.broadcasted_iota(jnp.int32, (1, LANES), 1) < HS, 1.0, 0.0)
    low_b, high_b = low.astype(bf16), (1.0 - low).astype(bf16)
    k_s[...] = kv_ref[:, :tok, :].reshape(span, LANES)
    values = kv_ref[:, tok:, :].reshape(span, LANES)
    v_s[0] = values * low_b + high_b
    v_s[1] = values * high_b + low_b


def other_half(head):
    return (LANES - 1, LANES - 2) if head == 0 else (0, 1)


def first_kernel(kv_ref, q_ref, sum_ref, k_s, v_s):
    groups, tok = q_ref.shape[0], q_ref.shape[1]
    stage_keys(kv_ref, k_s, v_s)
    lane = lax.broadcasted_iota(jnp.int32, (1, LANES), 1)
    for group in range(0, groups, 2):
        for head, top, sums in attend_blocks(q_ref, group, 2, k_s, v_s):
            sum_ref[head, pl.ds(group * tok, 2 * tok), :] = jnp.where(lane == other_half(head)[1], top, sums)


def second_kernel(kv_ref, q_ref, sum_ref, out_ref, k_s, v_s, o_s, extra_s, slot_s, slot_t, packed_s):
    groups, tok = q_ref.shape[0], q_ref.shape[1]
    slots, width = groups * SLOTS, groups * tok
    stage_keys(kv_ref, k_s, v_s)
    lane = lax.broadcasted_iota(jnp.int32, (tok, LANES), 1)
    lane_f = lane.astype(f32)
    for group in range(groups):
        rows = pl.ds(group * tok, tok)
        meta = q_ref[group, :, LANES:].astype(f32)
        tile, cell = meta[:, 0:1], meta[:, 2:3]
        place = meta[:, 1:2] + float(group * SLOTS)
        gain = meta[:, 3:4] + meta[:, 4:5]
        sums = []
        extra = jnp.where(lane_f == 96.0 + place, cell, 0.0)
        for head, top_b, sum_b in attend_blocks(q_ref, group, 1, k_s, v_s):
            at, top_at = other_half(head)
            sum_a = sum_ref[head, rows, :]
            top_a = sum_a[:, top_at : top_at + 1]
            top = jnp.maximum(top_a, top_b)
            o = sum_a * jnp.exp2(top_a - top) + sum_b * jnp.exp2(top_b - top)
            total = o[:, at : at + 1]
            sums.append(o * (gain / total))
            left = top + jnp.log2(total)
            for step in range(3):
                piece = left.astype(bf16).astype(f32)
                left = left - piece
                extra = jnp.where(lane_f == step * 32.0 + head * 16.0 + place, piece, extra)
        o_s[rows, :] = jnp.where(lane < HS, sums[0], sums[1]).astype(bf16)
        extra_s[rows, :] = extra.astype(bf16)
        slot_s[rows, :] = jnp.where(lane == 0, tile * PIECE + place, tile)
    slot_t[...] = jnp.transpose(slot_s[...])
    step = 16 * PIECE
    tiles = out_ref.shape[0] // PIECE
    for begin in range(0, out_ref.shape[0], step):
        row = (lax.broadcasted_iota(jnp.int32, (step, width), 0) + begin).astype(f32)
        main = jnp.where(row == slot_t[0:1, :], 1.0, 0.0).astype(bf16)
        packed_s[pl.ds(begin, step), :] = dot(main, o_s[...])
    row = lax.broadcasted_iota(jnp.int32, (tiles, width), 0).astype(f32)
    tail = jnp.where(row == slot_t[1:2, :], 1.0, 0.0).astype(bf16)
    packed_s[pl.ds(slots, tiles, stride=PIECE), :] = dot(tail, extra_s[...])
    out_ref[...] = packed_s[...].astype(bf16)


def attention_cost(queries, keys):
    return pl.CostEstimate(
        flops=2 * 2 * 2 * queries * keys * LANES, bytes_accessed=4 * queries * LANES, transcendentals=2 * queries * keys
    )


def attend_first(kv, q_all):
    blocks, tok2, _ = kv.shape
    groups, tok, _ = q_all.shape
    span, rows = blocks * tok2 // 2, groups * tok
    vmem = pl.BlockSpec(memory_space=pltpu.VMEM)
    return pl.pallas_call(
        first_kernel,
        out_shape=jax.ShapeDtypeStruct((2, rows, LANES), f32),
        in_specs=[vmem, vmem],
        out_specs=vmem,
        scratch_shapes=[pltpu.VMEM((span, LANES), bf16), pltpu.VMEM((2, span, LANES), bf16)],
        compiler_params=pltpu.CompilerParams(vmem_limit_bytes=16 * MIB),
        cost_estimate=attention_cost(rows, span),
        name="attend_own_core",
    )(kv, q_all)


def attend_second(kv, q_all, sums, tiles):
    blocks, tok2, _ = kv.shape
    groups, tok, _ = q_all.shape
    span, rows = blocks * tok2 // 2, groups * tok
    vmem = pl.BlockSpec(memory_space=pltpu.VMEM)
    return pl.pallas_call(
        second_kernel,
        out_shape=jax.ShapeDtypeStruct((tiles * PIECE, LANES), bf16),
        in_specs=[vmem] * 3,
        out_specs=vmem,
        scratch_shapes=[
            pltpu.VMEM((span, LANES), bf16),
            pltpu.VMEM((2, span, LANES), bf16),
            pltpu.VMEM((rows, LANES), bf16),
            pltpu.VMEM((rows, LANES), bf16),
            pltpu.VMEM((rows, LANES), f32),
            pltpu.VMEM((LANES, rows), f32),
            pltpu.VMEM((tiles * PIECE, LANES), f32),
        ],
        compiler_params=pltpu.CompilerParams(vmem_limit_bytes=16 * MIB),
        cost_estimate=attention_cost(rows, span),
        name="attend_other_core",
    )(kv, q_all, sums)


def splat_kernel(groups, _, x_ref, *refs):
    out_ref, x_s, y_s, r_s = refs[-4:]
    cells = out_ref.shape[1]
    sources = x_ref.shape[0] // PIECE
    slots = groups * SLOTS
    x_s[...] = x_ref[...].astype(f32)
    meta = x_s[pl.ds(slots, sources, stride=PIECE), :]
    lse = meta + pltpu.roll(meta, LANES - 32, 1) + pltpu.roll(meta, LANES - 64, 1)
    lse = lse.reshape(sources // (2 * groups), 2 * groups, LANES)
    turns = [lse] + [pltpu.roll(lse, 2 * k, 1) for k in range(1, groups)]
    top = functools.reduce(jnp.maximum, turns)
    powers = [jnp.exp2(t - top) for t in turns]
    weight = powers[0] / functools.reduce(jnp.add, powers)
    weight = weight.reshape(sources, LANES)
    lane = lax.broadcasted_iota(jnp.int32, (sources, LANES), 1)
    y_s[...] = jnp.zeros_like(y_s)
    y_s[:sources, :] = jnp.where(lane < 32, weight, meta)
    y_t = jnp.transpose(y_s[...])
    r_s[...] = jnp.zeros_like(r_s)
    for slot in range(slots):
        r_s[pl.ds(slot * LANES, sources), :] = x_s[pl.ds(slot, sources, stride=PIECE), :].astype(bf16)
    cell = (lax.broadcasted_iota(jnp.int32, (cells, LANES), 0) + 1).astype(f32)
    hits = [cell == y_t[96 + slot : 97 + slot, :] for slot in range(slots)]
    sums = []
    for head in range(2):
        spread = jnp.concatenate(
            [
                jnp.where(hits[slot], y_t[head * 16 + slot : head * 16 + slot + 1, :], 0.0).astype(bf16)
                for slot in range(slots)
            ],
            axis=1,
        )
        sums.append(dot(spread, r_s[...]))
    low = lax.broadcasted_iota(jnp.int32, (1, LANES), 1) < HS
    features = jnp.where(low, sums[0], sums[1]).astype(bf16)
    for copy in range(out_ref.shape[0]):
        out_ref[copy] = features


def splat(own, received, early, cells, groups, copies):
    rows = received.shape[0]
    return pl.pallas_call(
        functools.partial(splat_kernel, groups),
        out_shape=jax.ShapeDtypeStruct((copies, cells, LANES), bf16),
        in_specs=[pl.BlockSpec(memory_space=pltpu.SMEM), pl.BlockSpec(memory_space=pltpu.VMEM)]
        + [pl.BlockSpec(memory_space=pl.ANY)] * len(early),
        out_specs=pl.BlockSpec(memory_space=pltpu.VMEM),
        scratch_shapes=[
            pltpu.VMEM((rows, LANES), f32),
            pltpu.VMEM((LANES, LANES), f32),
            pltpu.VMEM((groups * SLOTS * LANES, LANES), bf16),
        ],
        compiler_params=pltpu.CompilerParams(vmem_limit_bytes=12 * MIB),
        name="join_splat",
    )(own, received, *early)


def mlp_kernel(own_ref, *refs):
    weights, (f_ref, base_hbm, gain_ref, up_ref, down_hbm) = refs[:4], refs[4:9]
    bev_ref, mix_ref, bev_s, base_s, down_s, sems = refs[9:]
    base_copy = pltpu.make_async_copy(base_hbm, base_s, sems.at[0])
    down_copy = pltpu.make_async_copy(down_hbm, down_s, sems.at[1])
    base_copy.start()
    down_copy.start()
    share = bev_ref.shape[0]
    own = own_ref[0]
    projected = None
    for k in range(0, len(weights), 2):
        features = jnp.concatenate([f_ref[own ^ k], f_ref[own ^ (k + 1)]], axis=1)
        term = dot(features, jnp.concatenate([weights[k][...], weights[k + 1][...]], axis=0))
        projected = term if projected is None else projected + term
    base_copy.wait()
    bev = base_s[...].astype(f32) + projected
    bev_s[...] = bev
    mean_square = jnp.mean(bev * bev, axis=1, keepdims=True)
    normed = (bev * lax.rsqrt(mean_square + 1e-06) * gain_ref[...]).astype(bf16)
    bev_ref[...] = bev_s[pl.ds(pl.multiple_of(own * share, share), share), :]
    step = up_ref.shape[1] // MLP_STEPS
    mixed = None
    for begin in range(0, up_ref.shape[1], step):
        u = dot(normed, up_ref[:, begin : begin + step])
        hidden = (0.5 * u * (1.0 + lax.erf(u * math.sqrt(0.5)))).astype(bf16)
        if begin == 0:
            down_copy.wait()
        term = dot(hidden, down_s[begin : begin + step, :])
        mixed = term if mixed is None else mixed + term
    mix_ref[...] = mixed.astype(bf16)


def mlp(own, weights, features, base, gain, up, down):
    heads = features.shape[0]
    cells, width = base.shape
    vmem, hbm = pl.BlockSpec(memory_space=pltpu.VMEM), pl.BlockSpec(memory_space=pltpu.HBM)
    return pl.pallas_call(
        mlp_kernel,
        out_shape=(
            jax.ShapeDtypeStruct((cells // heads, width), f32),
            jax.ShapeDtypeStruct((cells, width), bf16),
        ),
        in_specs=[pl.BlockSpec(memory_space=pltpu.SMEM)] + [vmem] * 5 + [hbm, vmem, vmem, hbm],
        out_specs=(vmem, vmem),
        scratch_shapes=[
            pltpu.VMEM((cells, width), f32),
            pltpu.VMEM((cells, width), bf16),
            pltpu.VMEM(down.shape, bf16),
            pltpu.SemaphoreType.DMA((2,)),
        ],
        compiler_params=pltpu.CompilerParams(vmem_limit_bytes=20 * MIB),
        name="project_mlp",
    )(
        own,
        *weights,
        features,
        pltpu.with_memory_space_constraint(base, pltpu.HBM),
        gain,
        up,
        pltpu.with_memory_space_constraint(down, pltpu.HBM),
    )


def swap(x, axis, bit):
    return lax.ppermute(x, axis, [(i, i ^ bit) for i in range(lax.axis_size(axis))])


def body(
    queries,
    key_states,
    value_states,
    splat_weight,
    tile_of,
    cell_of,
    bev_base,
    norm_gain,
    out_weight,
    up_weight,
    down_weight,
):
    tok = queries.shape[1]
    tiles = lax.axis_size("z") * lax.axis_size("y") * lax.axis_size("core")
    groups = lax.axis_size("y")
    heads = lax.axis_size("head")
    cells = bev_base.shape[1]
    q_copies, kv = prologue(
        queries, key_states, value_states, tile_of.reshape(1, tok), cell_of, splat_weight, groups
    )
    q_all = lax.all_to_all(q_copies, "y", 0, 0)
    own_kv = lax.all_gather(kv, "z")
    own_kv, q_all = lax.optimization_barrier((own_kv, q_all))
    other_kv = swap(own_kv, "core", 1)
    sums = attend_first(own_kv, q_all)
    packed = attend_second(other_kv, q_all, sums, tiles)
    packed, out_weight = lax.optimization_barrier((packed, out_weight))
    weights = tuple(swap(out_weight, "head", k) for k in range(heads - 1, 0, -1))[::-1]
    received = lax.all_to_all(packed.reshape(tiles, PIECE // 2, 2, LANES), ("z", "y", "core"), 0, 0)
    own = lax.axis_index("head").astype(jnp.int32).reshape(1)
    features = splat(own, received.reshape(tiles * PIECE, LANES), weights, cells, groups, heads)
    features = lax.all_to_all(features, "head", 0, 0)
    bev_rows, mixed = mlp(
        own, (out_weight,) + weights, features, bev_base[0], norm_gain[None, :], up_weight, down_weight
    )
    mixed = lax.all_to_all(mixed.reshape(heads, cells // heads, mixed.shape[1]), "head", 0, 0)
    return (bev_rows + jnp.sum(mixed.astype(f32), axis=0)).astype(bf16)[None]


def solution(mesh):
    core, y = 2, 4
    z = mesh.shape["ctx"] // (core * y)
    split = Mesh(
        mesh.devices.reshape(z, y, core, mesh.shape["head"], mesh.shape["scene"]),
        ("z", "y", "core", "head", "scene"),
    )
    ctx = ("z", "y", "core")
    placed = (
        P("scene", ctx, "head"),
        P("scene", ctx, "head"),
        P("scene", ctx, "head"),
        P("scene", ctx),
        P("scene", ctx, None),
        P("scene", ctx),
        P("scene", ctx, None),
        P(),
        P("head", None),
        P(None, "head"),
        P("head", None),
    )
    return jax.shard_map(
        body,
        mesh=split,
        in_specs=placed,
        out_specs=P("scene", ctx + ("head",), None),
        check_vma=False,
    )
```

```python
import functools
import math

import jax
import jax.numpy as jnp
from jax import lax
from jax.experimental import pallas as pl
from jax.experimental.pallas import tpu as pltpu
from jax.sharding import Mesh
from jax.sharding import PartitionSpec as P

HS = 64
LANES = 128
SLOTS = 4
PIECE = 18
EXPONENT = math.log2(math.e) / math.sqrt(HS)
MIB = 1024 * 1024
MLP_STEPS = 2

f32 = jnp.float32
bf16 = jnp.bfloat16


def dot(a, b):
    return lax.dot_general(a, b, (((1,), (0,)), ((), ())), preferred_element_type=f32)


def dot_nt(a, b):
    return lax.dot_general(a, b, (((1,), (1,)), ((), ())), preferred_element_type=f32)


def prologue_kernel(q_ref, k_ref, v_ref, tile_ref, cell_ref, splat_ref, q_out, kv_out, rows_s):
    copies, tok = q_out.shape[0], q_out.shape[1]
    tile = tile_ref[...].astype(f32)
    coarse = splat_ref[...].astype(bf16).astype(f32)
    rows_s[...] = jnp.zeros_like(rows_s)
    rows_s[0:1, :tok] = tile
    rows_s[2:3, :tok] = (cell_ref[...] + 1).astype(f32)
    rows_s[3:4, :tok] = coarse
    rows_s[4:5, :tok] = splat_ref[...] - coarse
    columns = jnp.transpose(rows_s[...])[:tok, :]
    shape = (tok, tok)
    earlier = lax.broadcasted_iota(jnp.int32, shape, 1) < lax.broadcasted_iota(jnp.int32, shape, 0)
    alike = jnp.where(columns[:, 0:1] == tile, 1.0, 0.0)
    rank = jnp.sum(jnp.where(earlier, alike, 0.0), axis=1, keepdims=True)
    lane = lax.broadcasted_iota(jnp.int32, (tok, LANES), 1)
    meta = jnp.where(lane == 1, rank, columns).astype(bf16)
    for copy in range(copies):
        q_out[copy, :, :LANES] = q_ref[0]
        q_out[copy, :, LANES:] = meta
    kv_out[:tok, :] = k_ref[0]
    kv_out[tok:, :] = v_ref[0]


def prologue(queries, key_states, value_states, tile, cell, splat_weight, copies):
    tok = queries.shape[1]
    vmem = pl.BlockSpec(memory_space=pltpu.VMEM)
    return pl.pallas_call(
        prologue_kernel,
        out_shape=(
            jax.ShapeDtypeStruct((copies, tok, 2 * LANES), bf16),
            jax.ShapeDtypeStruct((2 * tok, LANES), bf16),
        ),
        in_specs=[vmem] * 6,
        out_specs=(vmem, vmem),
        scratch_shapes=[pltpu.VMEM((LANES, 2 * LANES), f32)],
        compiler_params=pltpu.CompilerParams(vmem_limit_bytes=58 * MIB),
        name="prologue",
    )(queries, key_states, value_states, tile, cell, splat_weight)


def attend_blocks(q_ref, first, count, k_s, v_s):
    low = lax.broadcasted_iota(jnp.int32, (1, LANES), 1) < HS
    q = jnp.concatenate([q_ref[first + i, :, :LANES] for i in range(count)], axis=0)
    rows, span, step = q.shape[0], k_s.shape[0], 640
    keeps = [jnp.where(low if head == 0 else ~low, 1.0, 0.0).astype(bf16) for head in range(2)]
    s = dot_nt(jnp.concatenate([q * keep for keep in keeps], axis=0), k_s[...])
    top = jnp.max(s, axis=1, keepdims=True)
    sums = [None, None]
    for begin in range(0, span, step):
        p = jnp.exp2((s[:, begin : begin + step] - top) * EXPONENT).astype(bf16)
        for head in range(2):
            term = dot(p[head * rows : (head + 1) * rows], v_s[head, begin : begin + step, :])
            sums[head] = term if sums[head] is None else sums[head] + term
    return [(head, top[head * rows : (head + 1) * rows] * EXPONENT, sums[head]) for head in range(2)]


def stage_keys(kv_ref, k_s, v_s):
    blocks, tok = kv_ref.shape[0], kv_ref.shape[1] // 2
    span = blocks * tok
    low = jnp.where(lax.broadcasted_iota(jnp.int32, (1, LANES), 1) < HS, 1.0, 0.0)
    low_b, high_b = low.astype(bf16), (1.0 - low).astype(bf16)
    k_s[...] = kv_ref[:, :tok, :].reshape(span, LANES)
    values = kv_ref[:, tok:, :].reshape(span, LANES)
    v_s[0] = values * low_b + high_b
    v_s[1] = values * high_b + low_b


def other_half(head):
    return (LANES - 1, LANES - 2) if head == 0 else (0, 1)


def first_kernel(kv_ref, q_ref, sum_ref, k_s, v_s):
    groups, tok = q_ref.shape[0], q_ref.shape[1]
    stage_keys(kv_ref, k_s, v_s)
    lane = lax.broadcasted_iota(jnp.int32, (1, LANES), 1)
    for group in range(0, groups, 2):
        for head, top, sums in attend_blocks(q_ref, group, 2, k_s, v_s):
            sum_ref[head, pl.ds(group * tok, 2 * tok), :] = jnp.where(lane == other_half(head)[1], top, sums)


def second_kernel(kv_ref, q_ref, sum_ref, out_ref, k_s, v_s, o_s, extra_s, slot_s, slot_t, packed_s):
    groups, tok = q_ref.shape[0], q_ref.shape[1]
    slots, width = groups * SLOTS, groups * tok
    stage_keys(kv_ref, k_s, v_s)
    lane = lax.broadcasted_iota(jnp.int32, (tok, LANES), 1)
    lane_f = lane.astype(f32)
    for group in range(groups):
        rows = pl.ds(group * tok, tok)
        meta = q_ref[group, :, LANES:].astype(f32)
        tile, cell = meta[:, 0:1], meta[:, 2:3]
        place = meta[:, 1:2] + float(group * SLOTS)
        gain = meta[:, 3:4] + meta[:, 4:5]
        sums = []
        extra = jnp.where(lane_f == 96.0 + place, cell, 0.0)
        for head, top_b, sum_b in attend_blocks(q_ref, group, 1, k_s, v_s):
            at, top_at = other_half(head)
            sum_a = sum_ref[head, rows, :]
            top_a = sum_a[:, top_at : top_at + 1]
            top = jnp.maximum(top_a, top_b)
            o = sum_a * jnp.exp2(top_a - top) + sum_b * jnp.exp2(top_b - top)
            total = o[:, at : at + 1]
            sums.append(o * (gain / total))
            left = top + jnp.log2(total)
            for step in range(3):
                piece = left.astype(bf16).astype(f32)
                left = left - piece
                extra = jnp.where(lane_f == step * 32.0 + head * 16.0 + place, piece, extra)
        o_s[rows, :] = jnp.where(lane < HS, sums[0], sums[1]).astype(bf16)
        extra_s[rows, :] = extra.astype(bf16)
        slot_s[rows, :] = jnp.where(lane == 0, tile * PIECE + place, tile)
    slot_t[...] = jnp.transpose(slot_s[...])
    step = 16 * PIECE
    tiles = out_ref.shape[0] // PIECE
    for begin in range(0, out_ref.shape[0], step):
        row = (lax.broadcasted_iota(jnp.int32, (step, width), 0) + begin).astype(f32)
        main = jnp.where(row == slot_t[0:1, :], 1.0, 0.0).astype(bf16)
        packed_s[pl.ds(begin, step), :] = dot(main, o_s[...])
    row = lax.broadcasted_iota(jnp.int32, (tiles, width), 0).astype(f32)
    tail = jnp.where(row == slot_t[1:2, :], 1.0, 0.0).astype(bf16)
    packed_s[pl.ds(slots, tiles, stride=PIECE), :] = dot(tail, extra_s[...])
    out_ref[...] = packed_s[...].astype(bf16)


def attention_cost(queries, keys):
    return pl.CostEstimate(
        flops=2 * 2 * 2 * queries * keys * LANES, bytes_accessed=4 * queries * LANES, transcendentals=2 * queries * keys
    )


def attend_first(kv, q_all):
    blocks, tok2, _ = kv.shape
    groups, tok, _ = q_all.shape
    span, rows = blocks * tok2 // 2, groups * tok
    vmem = pl.BlockSpec(memory_space=pltpu.VMEM)
    return pl.pallas_call(
        first_kernel,
        out_shape=jax.ShapeDtypeStruct((2, rows, LANES), f32),
        in_specs=[vmem, vmem],
        out_specs=vmem,
        scratch_shapes=[pltpu.VMEM((span, LANES), bf16), pltpu.VMEM((2, span, LANES), bf16)],
        compiler_params=pltpu.CompilerParams(vmem_limit_bytes=16 * MIB),
        cost_estimate=attention_cost(rows, span),
        name="attend_own_core",
    )(kv, q_all)


def attend_second(kv, q_all, sums, tiles):
    blocks, tok2, _ = kv.shape
    groups, tok, _ = q_all.shape
    span, rows = blocks * tok2 // 2, groups * tok
    vmem = pl.BlockSpec(memory_space=pltpu.VMEM)
    return pl.pallas_call(
        second_kernel,
        out_shape=jax.ShapeDtypeStruct((tiles * PIECE, LANES), bf16),
        in_specs=[vmem] * 3,
        out_specs=vmem,
        scratch_shapes=[
            pltpu.VMEM((span, LANES), bf16),
            pltpu.VMEM((2, span, LANES), bf16),
            pltpu.VMEM((rows, LANES), bf16),
            pltpu.VMEM((rows, LANES), bf16),
            pltpu.VMEM((rows, LANES), f32),
            pltpu.VMEM((LANES, rows), f32),
            pltpu.VMEM((tiles * PIECE, LANES), f32),
        ],
        compiler_params=pltpu.CompilerParams(vmem_limit_bytes=16 * MIB),
        cost_estimate=attention_cost(rows, span),
        name="attend_other_core",
    )(kv, q_all, sums)


def splat_kernel(groups, _, x_ref, *refs):
    out_ref, x_s, y_s, r_s = refs[-4:]
    cells = out_ref.shape[1]
    sources = x_ref.shape[0] // PIECE
    slots = groups * SLOTS
    x_s[...] = x_ref[...].astype(f32)
    meta = x_s[pl.ds(slots, sources, stride=PIECE), :]
    lse = meta + pltpu.roll(meta, LANES - 32, 1) + pltpu.roll(meta, LANES - 64, 1)
    lse = lse.reshape(sources // (2 * groups), 2 * groups, LANES)
    turns = [lse] + [pltpu.roll(lse, 2 * k, 1) for k in range(1, groups)]
    top = functools.reduce(jnp.maximum, turns)
    powers = [jnp.exp2(t - top) for t in turns]
    weight = powers[0] / functools.reduce(jnp.add, powers)
    weight = weight.reshape(sources, LANES)
    lane = lax.broadcasted_iota(jnp.int32, (sources, LANES), 1)
    y_s[...] = jnp.zeros_like(y_s)
    y_s[:sources, :] = jnp.where(lane < 32, weight, meta)
    y_t = jnp.transpose(y_s[...])
    r_s[...] = jnp.zeros_like(r_s)
    for slot in range(slots):
        r_s[pl.ds(slot * LANES, sources), :] = x_s[pl.ds(slot, sources, stride=PIECE), :].astype(bf16)
    cell = (lax.broadcasted_iota(jnp.int32, (cells, LANES), 0) + 1).astype(f32)
    hits = [cell == y_t[96 + slot : 97 + slot, :] for slot in range(slots)]
    sums = []
    for head in range(2):
        spread = jnp.concatenate(
            [
                jnp.where(hits[slot], y_t[head * 16 + slot : head * 16 + slot + 1, :], 0.0).astype(bf16)
                for slot in range(slots)
            ],
            axis=1,
        )
        sums.append(dot(spread, r_s[...]))
    low = lax.broadcasted_iota(jnp.int32, (1, LANES), 1) < HS
    features = jnp.where(low, sums[0], sums[1]).astype(bf16)
    for copy in range(out_ref.shape[0]):
        out_ref[copy] = features


def splat(own, received, early, cells, groups, copies):
    rows = received.shape[0]
    return pl.pallas_call(
        functools.partial(splat_kernel, groups),
        out_shape=jax.ShapeDtypeStruct((copies, cells, LANES), bf16),
        in_specs=[pl.BlockSpec(memory_space=pltpu.SMEM), pl.BlockSpec(memory_space=pltpu.VMEM)]
        + [pl.BlockSpec(memory_space=pl.ANY)] * len(early),
        out_specs=pl.BlockSpec(memory_space=pltpu.VMEM),
        scratch_shapes=[
            pltpu.VMEM((rows, LANES), f32),
            pltpu.VMEM((LANES, LANES), f32),
            pltpu.VMEM((groups * SLOTS * LANES, LANES), bf16),
        ],
        compiler_params=pltpu.CompilerParams(vmem_limit_bytes=12 * MIB),
        name="join_splat",
    )(own, received, *early)


def mlp_kernel(own_ref, *refs):
    weights, (f_ref, base_ref, gain_ref, up_ref, down_hbm) = refs[:4], refs[4:9]
    bev_ref, mix_ref, bev_s, own_s, down_s, sems = refs[9:]
    own_copy = pltpu.make_async_copy(weights[0], own_s, sems.at[0])
    down_copy = pltpu.make_async_copy(down_hbm, down_s, sems.at[1])
    own_copy.start()
    down_copy.start()
    share = bev_ref.shape[0]
    own = own_ref[0]
    rows = [own_s] + list(weights[1:])
    projected = None
    for k in range(len(rows) - 2, -1, -2):
        if k == 0:
            own_copy.wait()
        features = jnp.concatenate([f_ref[own ^ k], f_ref[own ^ (k + 1)]], axis=1)
        term = dot(features, jnp.concatenate([rows[k][...], rows[k + 1][...]], axis=0))
        projected = term if projected is None else projected + term
    bev = base_ref[...].astype(f32) + projected
    bev_s[...] = bev
    mean_square = jnp.mean(bev * bev, axis=1, keepdims=True)
    normed = (bev * lax.rsqrt(mean_square + 1e-06) * gain_ref[...]).astype(bf16)
    bev_ref[...] = bev_s[pl.ds(pl.multiple_of(own * share, share), share), :]
    step = up_ref.shape[1] // MLP_STEPS
    mixed = None
    for begin in range(0, up_ref.shape[1], step):
        u = dot(normed, up_ref[:, begin : begin + step])
        hidden = (0.5 * u * (1.0 + lax.erf(u * math.sqrt(0.5)))).astype(bf16)
        if begin == 0:
            down_copy.wait()
        term = dot(hidden, down_s[begin : begin + step, :])
        mixed = term if mixed is None else mixed + term
    mix_ref[...] = mixed.astype(bf16)


def mlp(own, weights, features, base, gain, up, down):
    heads = features.shape[0]
    cells, width = base.shape
    vmem, hbm = pl.BlockSpec(memory_space=pltpu.VMEM), pl.BlockSpec(memory_space=pltpu.HBM)
    return pl.pallas_call(
        mlp_kernel,
        out_shape=(
            jax.ShapeDtypeStruct((cells // heads, width), f32),
            jax.ShapeDtypeStruct((cells, width), bf16),
        ),
        in_specs=[pl.BlockSpec(memory_space=pltpu.SMEM)] + [hbm] + [vmem] * 7 + [hbm],
        out_specs=(vmem, vmem),
        scratch_shapes=[
            pltpu.VMEM((cells, width), f32),
            pltpu.VMEM(weights[0].shape, bf16),
            pltpu.VMEM(down.shape, bf16),
            pltpu.SemaphoreType.DMA((2,)),
        ],
        compiler_params=pltpu.CompilerParams(vmem_limit_bytes=20 * MIB),
        name="project_mlp",
    )(
        own,
        pltpu.with_memory_space_constraint(weights[0], pltpu.HBM),
        *weights[1:],
        features,
        base,
        gain,
        up,
        pltpu.with_memory_space_constraint(down, pltpu.HBM),
    )


def swap(x, axis, bit):
    return lax.ppermute(x, axis, [(i, i ^ bit) for i in range(lax.axis_size(axis))])


def body(
    queries,
    key_states,
    value_states,
    splat_weight,
    tile_of,
    cell_of,
    bev_base,
    norm_gain,
    out_weight,
    up_weight,
    down_weight,
):
    tok = queries.shape[1]
    tiles = lax.axis_size("z") * lax.axis_size("y") * lax.axis_size("core")
    groups = lax.axis_size("y")
    heads = lax.axis_size("head")
    cells = bev_base.shape[1]
    q_copies, kv = prologue(
        queries, key_states, value_states, tile_of.reshape(1, tok), cell_of, splat_weight, groups
    )
    q_all = lax.all_to_all(q_copies, "y", 0, 0)
    own_kv = lax.all_gather(kv, "z")
    own_kv, q_all = lax.optimization_barrier((own_kv, q_all))
    other_kv = swap(own_kv, "core", 1)
    sums = attend_first(own_kv, q_all)
    packed = attend_second(other_kv, q_all, sums, tiles)
    packed, out_weight = lax.optimization_barrier((packed, out_weight))
    weights = tuple(swap(out_weight, "head", k) for k in range(heads - 1, 0, -1))[::-1]
    received = lax.all_to_all(packed.reshape(tiles, PIECE // 2, 2, LANES), ("z", "y", "core"), 0, 0)
    own = lax.axis_index("head").astype(jnp.int32).reshape(1)
    features = splat(own, received.reshape(tiles * PIECE, LANES), weights, cells, groups, heads)
    features = lax.all_to_all(features, "head", 0, 0)
    bev_rows, mixed = mlp(
        own, (out_weight,) + weights, features, bev_base[0], norm_gain[None, :], up_weight, down_weight
    )
    mixed = lax.all_to_all(mixed.reshape(heads, cells // heads, mixed.shape[1]), "head", 0, 0)
    return (bev_rows + jnp.sum(mixed.astype(f32), axis=0)).astype(bf16)[None]


def solution(mesh):
    core, y = 2, 4
    z = mesh.shape["ctx"] // (core * y)
    split = Mesh(
        mesh.devices.reshape(z, y, core, mesh.shape["head"], mesh.shape["scene"]),
        ("z", "y", "core", "head", "scene"),
    )
    ctx = ("z", "y", "core")
    placed = (
        P("scene", ctx, "head"),
        P("scene", ctx, "head"),
        P("scene", ctx, "head"),
        P("scene", ctx),
        P("scene", ctx, None),
        P("scene", ctx),
        P("scene", ctx, None),
        P(),
        P("head", None),
        P(None, "head"),
        P("head", None),
    )
    return jax.shard_map(
        body,
        mesh=split,
        in_specs=placed,
        out_specs=P("scene", ctx + ("head",), None),
        check_vma=False,
    )
```
